512 devices in a mesh: section: 8 (over y_hi, x), dp: 64 (over z, y_lo, core).
Axes of the slice: x: 4, y: 4 (y_hi: 2, y_lo: 2; y = y_hi * 2 + y_lo), z: 16, core: 2. Of those that a mesh axis runs over, the one named last changes fastest.
Arguments:
- inputs: bfloat16 [4, 2048, 4096], P(None, 'dp'), may hold values from -6 to 6
- out_grad: bfloat16 [4, 2048, 4096], P(None, 'dp'), may hold values from -6 to 6
- doc_ids: int32 [4, 2048], P(None, 'dp'), may hold values from 0 to 255, never falling along the last dimension, each value on 1 to 16 neighbouring positions
- query_weight: bfloat16 [8, 4096, 512], P('section', 'dp'), may hold values from -0.09375 to 0.09375
- out_weight: bfloat16 [8, 4096, 512], P('section', 'dp'), may hold values from -0.25 to 0.25
- master: float32 [8, 2, 4096, 128], P('section', None, 'dp'), may hold values from -0.09375 to 0.09375
- first_moment: float32 [8, 2, 4096, 128], P('section', None, 'dp'), may hold values from -0.00390625 to 0.00390625
- second_moment: float32 [8, 2, 4096, 128], P('section', None, 'dp'), may hold values from 1e-08 to 1e-06
Outputs:
- update: float32 [8, 2, 4096, 128], P('section', None, 'dp')
- new_weights: bfloat16 [8, 2, 4096, 128], P('section', None, 'dp')
The draws below stay inside these ranges and needn't reach their ends.
Inputs may be any that keep to these rules, and one draw needn't show every extreme that they name: `doc_ids`: ids never fall along a row; each id covers 1 to 16 consecutive positions.
All inputs are finite; a program needn't handle non-finite values.
Results may differ from the reference program's by a relative error of at most 0.02.
Values may be sent and summed in bfloat16 or wider, within the bound.
No kernel may reach another device: no remote copies, remote signals or barrier semaphores. Data moves between devices by JAX's collectives and lax.ppermute only.
A program may use at most 128 MiB of HBM per device.

```python
import math
import jax
import jax.numpy as jnp
import numpy as np
from jax import lax

D = 4096
HEAD = 128
QH = 4
MICRO = 4
SEQ = 32
TOKENS = 2048
N_SECTION = 8
N_DP = 64


def level_of(own_key, shape, shards, smallest, largest):
    gain, own = 1.0, jax.random.fold_in(own_key, 6)
    for axis_at, shards_of in shards:
        steps = jnp.exp(jax.random.uniform(jax.random.fold_in(own, axis_at), (shards_of,), jnp.float32, smallest / len(shards), largest / len(shards)))
        gain = gain * jnp.repeat(steps, shape[axis_at] // shards_of).reshape([-1 if axis == axis_at else 1 for axis in range(len(shape))])
    return gain


def profile(count, total, reach, skew):
    portions = [(1 << 20) // math.isqrt(grade ** skew) + 1 for grade in range(2, count + 1)]
    rest, given = total - reach - (count - 1), [1] * (count - 1)
    while rest > 0:
        movable = [i for i in range(count - 1) if given[i] < reach]
        whole, remaining = sum([portions[i] for i in movable]), rest
        for i in movable:
            extra = min(reach - given[i], max(1, remaining * portions[i] // whole), rest)
            given[i] = given[i] + extra
            rest = rest - extra
    return np.array([reach] + given)


def ragged_sizes(rng, amount, total, reach, skew):
    if amount == 2:
        one = jax.random.randint(rng, (), max(1, total - reach), min(reach, total - 1) + 1)
        return jnp.stack([one, total - one])
    lengths = jnp.asarray(profile(amount, total, reach, skew), jnp.int32)
    couples = (amount - 1) // 2
    donor, receiver = lengths[1:1 + 2 * couples:2], lengths[2:2 + 2 * couples:2]
    margin = jnp.minimum(donor - 1, reach - receiver)
    shifted = jax.random.randint(jax.random.fold_in(rng, 1), (couples,), 0, 1 << 20) % (margin + 1)
    lengths = lengths.at[1:1 + 2 * couples:2].set(donor - shifted).at[2:2 + 2 * couples:2].set(receiver + shifted)
    return lengths[jax.random.permutation(jax.random.fold_in(rng, 2), amount)]


def gaussian(own_key, dims, width, reach, split=(), kind=jnp.bfloat16):
    result = width * jax.random.normal(own_key, dims, jnp.float32)
    if split:
        result = result * level_of(own_key, dims, split, -0.22, 0.18)
    return jnp.clip(result, -reach, reach).astype(kind)


def setup_inputs(seed: int = 0) -> dict:
    key_list = jax.random.split(jax.random.key(seed), 9)
    inputs = gaussian(key_list[0], (MICRO, TOKENS, D), 1.0, 6.0, ((1, 64),))
    out_grad = gaussian(key_list[1], (MICRO, TOKENS, D), 1.0, 6.0, ((1, 64),))
    doc_ids = jax.vmap(lambda own: jnp.searchsorted(jnp.cumsum(ragged_sizes(own, TOKENS // 8, TOKENS, 16, 2)), jnp.arange(TOKENS), side="right"))(jax.random.split(key_list[2], MICRO)).reshape((MICRO, TOKENS)).astype(jnp.int32)
    query_weight = gaussian(key_list[3], (N_SECTION, D, QH * HEAD), D ** -0.5, 0.09375, ((0, 8), (1, 64)))
    out_weight = gaussian(key_list[4], (N_SECTION, D, QH * HEAD), (QH * HEAD) ** -0.5, 0.25, ((0, 8), (1, 64)))
    master = gaussian(key_list[5], (N_SECTION, 2, D, HEAD), D ** -0.5, 0.09375, ((0, 8), (2, 64)), jnp.float32)
    first_moment = gaussian(key_list[6], (N_SECTION, 2, D, HEAD), 0.0003, 0.00390625, ((0, 8), (2, 64)), jnp.float32)
    second_moment = jnp.clip(jnp.exp(math.log(9.999999974752427e-07) - 4.6051702 * jax.random.uniform(key_list[7], (N_SECTION, 2, D, HEAD), jnp.float32) ** level_of(key_list[7], (N_SECTION, 2, D, HEAD), ((0, 8), (2, 64)), -0.2, 0.2)), 9.99999993922529e-09, 9.999999974752427e-07)
    return dict(inputs=inputs, out_grad=out_grad, doc_ids=doc_ids, query_weight=query_weight, out_weight=out_weight, master=master, first_moment=first_moment, second_moment=second_moment)


NORM_EPS = 1e-05
BETA_FIRST = 0.9
BETA_SECOND = 0.95
ADAM_EPSILON = 1e-08
LEARN_RATE = 0.001
CLIP_NORM = 1.0

def widen(array):
    return lax.optimization_barrier(array).astype(jnp.float32)

def forward_parts(layer_in, allowed, w_query, w_keys, w_values, w_out):
    score_scale = 1.0 / math.sqrt(HEAD)
    count, length = (layer_in.shape[0], layer_in.shape[1])
    signal = layer_in.astype(jnp.float32)
    inverse = lax.rsqrt(lax.optimization_barrier(jnp.mean(signal * signal, axis=-1, keepdims=True)) + NORM_EPS)
    normed = (signal * inverse).astype(jnp.bfloat16)
    normed_wide = widen(normed)
    query_rows = jnp.einsum('bld,dh->blh', normed_wide, w_query.astype(jnp.float32)).astype(jnp.bfloat16)
    key_rows = jnp.einsum('bld,dh->blh', normed_wide, w_keys.astype(jnp.float32)).astype(jnp.bfloat16)
    values = jnp.einsum('bld,dh->blh', normed_wide, w_values.astype(jnp.float32)).astype(jnp.bfloat16)
    stacked_query = query_rows.reshape(count, length * QH, HEAD)
    mask = jnp.repeat(allowed, QH, axis=1)
    scores = jnp.einsum('bih,bjh->bij', widen(stacked_query), widen(key_rows)) * score_scale
    exp_scores = jnp.where(mask, jnp.exp(scores), 0.0)
    attn_probs = exp_scores / lax.optimization_barrier(jnp.sum(exp_scores, axis=-1, keepdims=True))
    attn_low = attn_probs.astype(jnp.bfloat16)
    context_heads = jnp.einsum('bij,bjh->bih', widen(attn_low), widen(values)).astype(jnp.bfloat16)
    context = context_heads.reshape(count, length, QH * HEAD)
    branch = jnp.einsum('blh,dh->bld', widen(context), w_out.astype(jnp.float32))
    return (signal, inverse, normed, stacked_query, key_rows, values, attn_probs, attn_low, context, branch)

def backward_parts(layer_in, allowed, upstream, w_query, w_keys, w_values, w_out):
    score_scale = 1.0 / math.sqrt(HEAD)
    count, length = (layer_in.shape[0], layer_in.shape[1])
    parts = forward_parts(layer_in, allowed, w_query, w_keys, w_values, w_out)
    signal, inverse, normed, stacked_query, key_rows, values, attn_probs, attn_low, context, branch = parts
    up_wide = widen(upstream)
    grad_context = jnp.einsum('bld,dh->blh', up_wide, w_out.astype(jnp.float32)).astype(jnp.bfloat16)
    context_grad_heads = grad_context.reshape(count, length * QH, HEAD)
    grad_probs = jnp.einsum('bih,bjh->bij', widen(context_grad_heads), widen(values))
    grad_values = jnp.einsum('bij,bih->bjh', widen(attn_low), widen(context_grad_heads)).astype(jnp.bfloat16)
    centred = grad_probs - lax.optimization_barrier(jnp.sum(attn_probs * grad_probs, axis=-1, keepdims=True))
    grad_scores = (attn_probs * centred * score_scale).astype(jnp.bfloat16)
    grad_query_heads = jnp.einsum('bij,bjh->bih', widen(grad_scores), widen(key_rows)).astype(jnp.bfloat16)
    grad_query = grad_query_heads.reshape(count, length, QH * HEAD)
    grad_keys = jnp.einsum('bij,bih->bjh', widen(grad_scores), widen(stacked_query)).astype(jnp.bfloat16)
    grad_normed = jnp.einsum('blh,dh->bld', widen(grad_query), w_query.astype(jnp.float32))
    grad_normed = grad_normed + jnp.einsum('blh,dh->bld', widen(grad_keys), w_keys.astype(jnp.float32))
    grad_normed = grad_normed + jnp.einsum('blh,dh->bld', widen(grad_values), w_values.astype(jnp.float32))
    grad_signal = inverse * grad_normed - signal * inverse ** 3 * lax.optimization_barrier(jnp.mean(grad_normed * signal, axis=-1, keepdims=True))
    grad_input = (up_wide + grad_signal).astype(jnp.bfloat16)
    grad_k = jnp.einsum('bld,blh->dh', widen(normed), widen(grad_keys))
    grad_v = jnp.einsum('bld,blh->dh', widen(normed), widen(grad_values))
    return (grad_input, jnp.stack([grad_k, grad_v]))

def reference(inputs, out_grad, doc_ids, query_weight, out_weight, master, first_moment, second_moment):
    count = MICRO * N_DP
    layer_in = inputs.reshape(count, SEQ, D)
    segment = doc_ids.reshape(count, SEQ)
    row_ids = lax.broadcasted_iota(jnp.int32, (SEQ, SEQ), 0)
    col_ids = lax.broadcasted_iota(jnp.int32, (SEQ, SEQ), 1)
    allowed = (segment[:, :, None] == segment[:, None, :]) & (col_ids <= row_ids)[None]
    low_master = master.astype(jnp.bfloat16)
    stored = []
    for layer in range(N_SECTION):
        stored.append(layer_in)
        parts = forward_parts(layer_in, allowed, query_weight[layer], low_master[layer, 0], low_master[layer, 1], out_weight[layer])
        layer_in = (parts[0] + parts[9]).astype(jnp.bfloat16)
    upstream = out_grad.reshape(count, SEQ, D)
    grads = [None] * N_SECTION
    for layer in range(N_SECTION - 1, -1, -1):
        upstream, grads[layer] = backward_parts(stored[layer], allowed, upstream, query_weight[layer], low_master[layer, 0], low_master[layer, 1], out_weight[layer])
    grad_full = jnp.stack(grads)
    total_sq = jnp.sum(grad_full * grad_full)
    factor = jnp.minimum(1.0, CLIP_NORM / jnp.sqrt(total_sq))
    clipped = grad_full * factor
    first_new = BETA_FIRST * first_moment + (1.0 - BETA_FIRST) * clipped
    second_new = BETA_SECOND * second_moment + (1.0 - BETA_SECOND) * clipped * clipped
    adam_step = first_new / (jnp.sqrt(second_new) + ADAM_EPSILON)
    fresh = (master - LEARN_RATE * adam_step).astype(jnp.bfloat16)
    return (adam_step, fresh)
```

```python
import functools
import math

import jax
import jax.numpy as jnp
from jax import lax
from jax.experimental import pallas as pl
from jax.experimental.pallas import tpu as pltpu
from jax.sharding import Mesh, PartitionSpec as P

NORM_EPS = 1e-05
BETA_FIRST = 0.9
BETA_SECOND = 0.95
ADAM_EPSILON = 1e-08
LEARN_RATE = 0.001
CLIP_NORM = 1.0

FINE = {"yh": 2, "x": 4, "z1": 4, "z2": 4, "yl": 2, "c": 2}
DP = ("z1", "z2", "yl", "c")
LAYERS = 4
LENGTH = 32
WIDTH = 4096
HEAD = 128
HEADS = 4
QW = HEAD * HEADS
KVW = QW + 2 * HEAD
COLS = KVW + QW
CHUNK = 1024
SCALE = 1.0 / math.sqrt(HEAD)
VMEM_LIMIT = 60 * 1024 * 1024
F32 = jnp.float32
BF16 = jnp.bfloat16


def dot_nn(a, b):
    return lax.dot_general(a, b, (((1,), (0,)), ((), ())), preferred_element_type=F32)


def dot_nt(a, b):
    return lax.dot_general(a, b, (((1,), (1,)), ((), ())), preferred_element_type=F32)


def dot_tn(a, b):
    return lax.dot_general(a, b, (((0,), (0,)), ((), ())), preferred_element_type=F32)


def weight_copies(w_hbm, w_vmem, sems, layer):
    copies = []
    for c in range(2):
        for yl in range(2):
            for z2 in range(4):
                at = (c * 2 + yl) * 4 + z2
                copies.append(
                    pltpu.make_async_copy(
                        w_hbm.at[:, z2, yl, c, layer], w_vmem.at[layer, at], sems.at[layer, at]
                    )
                )
    return copies


def stack_heads(rows):
    return jnp.concatenate([rows[:, h * HEAD : (h + 1) * HEAD] for h in range(HEADS)], axis=0)


def unstack_heads(rows):
    return jnp.concatenate([rows[h * LENGTH : (h + 1) * LENGTH] for h in range(HEADS)], axis=1)


def inverse_norm(h_ref, layer):
    total = jnp.zeros((LENGTH, 1), F32)
    for at in range(0, WIDTH, CHUNK):
        signal = h_ref[layer, :, at : at + CHUNK].astype(F32)
        total = total + jnp.sum(signal * signal, axis=-1, keepdims=True)
    return lax.rsqrt(total * (1.0 / WIDTH) + NORM_EPS)


def weight_rows(w_vmem, layer, at, first, last):
    per = CHUNK // 256
    block = w_vmem[layer, at // 256 : at // 256 + per, :, :, first:last]
    return block.reshape(CHUNK, last - first)


def forward_kernel(
    h_ref, seg_col, seg_row, w_hbm, out_ref, h_all, n_all, q_all, k_all, v_all, p_all, w_vmem, sems
):
    for layer in range(LAYERS):
        for copy in weight_copies(w_hbm, w_vmem, sems, layer):
            copy.start()
    row_ids = lax.broadcasted_iota(jnp.int32, (LENGTH, LENGTH), 0)
    col_ids = lax.broadcasted_iota(jnp.int32, (LENGTH, LENGTH), 1)
    allowed = ((seg_col[...] == seg_row[...]) & (col_ids <= row_ids)).astype(F32)
    mask = jnp.concatenate([allowed] * HEADS, axis=0) > 0.0
    h_all[0] = h_ref[...]
    for layer in range(LAYERS):
        inverse = inverse_norm(h_all, layer)
        for at in range(0, WIDTH, CHUNK):
            signal = h_all[layer, :, at : at + CHUNK].astype(F32)
            n_all[layer, :, at : at + CHUNK] = (signal * inverse).astype(BF16)
        for copy in weight_copies(w_hbm, w_vmem, sems, layer):
            copy.wait()
        acc = jnp.zeros((LENGTH, KVW), F32)
        for at in range(0, WIDTH, CHUNK):
            acc = acc + dot_nn(
                n_all[layer, :, at : at + CHUNK], weight_rows(w_vmem, layer, at, 0, KVW)
            )
        rows = acc.astype(BF16)
        query = stack_heads(rows[:, :QW])
        keys = rows[:, QW : QW + HEAD]
        values = rows[:, QW + HEAD :]
        scores = dot_nt(query, keys) * SCALE
        exp_scores = jnp.where(mask, jnp.exp(scores), 0.0)
        probs = exp_scores / jnp.sum(exp_scores, axis=-1, keepdims=True)
        context = unstack_heads(dot_nn(probs.astype(BF16), values).astype(BF16))
        q_all[layer] = query
        k_all[layer] = keys
        v_all[layer] = values
        p_all[layer] = probs
        for at in range(0, WIDTH, CHUNK):
            signal = h_all[layer, :, at : at + CHUNK].astype(F32)
            branch = dot_nt(context, weight_rows(w_vmem, layer, at, KVW, COLS))
            result = (signal + branch).astype(BF16)
            if layer + 1 < LAYERS:
                h_all[layer + 1, :, at : at + CHUNK] = result
            else:
                out_ref[:, at : at + CHUNK] = result


def backward_kernel(
    need_up, up_ref, h_all, q_all, k_all, v_all, p_all, w_hbm, out_ref, g_all, w_vmem, gn, sems
):
    for layer in reversed(range(LAYERS)):
        for copy in weight_copies(w_hbm, w_vmem, sems, layer):
            copy.start()
    out_ref[...] = up_ref[...]
    for layer in reversed(range(LAYERS)):
        for copy in weight_copies(w_hbm, w_vmem, sems, layer):
            copy.wait()
        acc = jnp.zeros((LENGTH, QW), F32)
        for at in range(0, WIDTH, CHUNK):
            acc = acc + dot_nn(
                out_ref[:, at : at + CHUNK], weight_rows(w_vmem, layer, at, KVW, COLS)
            )
        grad_context = stack_heads(acc.astype(BF16))
        query, keys, values, probs = q_all[layer], k_all[layer], v_all[layer], p_all[layer]
        grad_probs = dot_nt(grad_context, values)
        grad_values = dot_tn(probs.astype(BF16), grad_context).astype(BF16)
        centred = grad_probs - jnp.sum(probs * grad_probs, axis=-1, keepdims=True)
        grad_scores = (probs * centred * SCALE).astype(BF16)
        grad_query = unstack_heads(dot_nn(grad_scores, keys).astype(BF16))
        grad_keys = dot_tn(grad_scores, query).astype(BF16)
        g_all[layer, :, :HEAD] = grad_keys
        g_all[layer, :, HEAD:] = grad_values
        if layer == 0 and not need_up:
            continue
        grads = jnp.concatenate([grad_query, grad_keys, grad_values], axis=1)
        inverse = inverse_norm(h_all, layer)
        total = jnp.zeros((LENGTH, 1), F32)
        for at in range(0, WIDTH, CHUNK):
            part = dot_nt(grads, weight_rows(w_vmem, layer, at, 0, KVW))
            gn[:, at : at + CHUNK] = part
            signal = h_all[layer, :, at : at + CHUNK].astype(F32)
            total = total + jnp.sum(part * signal, axis=-1, keepdims=True)
        pull = inverse * inverse * inverse * (total * (1.0 / WIDTH))
        for at in range(0, WIDTH, CHUNK):
            signal = h_all[layer, :, at : at + CHUNK].astype(F32)
            upstream = out_ref[:, at : at + CHUNK].astype(F32)
            out_ref[:, at : at + CHUNK] = (
                upstream + inverse * gn[:, at : at + CHUNK] - signal * pull
            ).astype(BF16)


VM = pl.BlockSpec(memory_space=pltpu.VMEM)
ANY = pl.BlockSpec(memory_space=pl.ANY)
WEIGHT_SCRATCH = pltpu.VMEM((LAYERS, 16, 4, 64, COLS), BF16)
WEIGHT_SEMS = pltpu.SemaphoreType.DMA((LAYERS, 16))
STATE_SHAPES = (
    jax.ShapeDtypeStruct((LAYERS, LENGTH, WIDTH), BF16),
    jax.ShapeDtypeStruct((LAYERS, LENGTH, WIDTH), BF16),
    jax.ShapeDtypeStruct((LAYERS, LENGTH * HEADS, HEAD), BF16),
    jax.ShapeDtypeStruct((LAYERS, LENGTH, HEAD), BF16),
    jax.ShapeDtypeStruct((LAYERS, LENGTH, HEAD), BF16),
    jax.ShapeDtypeStruct((LAYERS, LENGTH * HEADS, LENGTH), F32),
)


def cost(products):
    return pl.CostEstimate(
        flops=products * 2 * LENGTH * WIDTH * COLS,
        bytes_accessed=LAYERS * WIDTH * COLS * 2,
        transcendentals=0,
    )


def run_forward(h, seg_col, seg_row, weights):
    return pl.pallas_call(
        forward_kernel,
        out_shape=(jax.ShapeDtypeStruct((LENGTH, WIDTH), BF16),) + STATE_SHAPES,
        in_specs=[VM, VM, VM, ANY],
        out_specs=(VM,) * 7,
        scratch_shapes=[WEIGHT_SCRATCH, WEIGHT_SEMS],
        compiler_params=pltpu.CompilerParams(vmem_limit_bytes=VMEM_LIMIT),
        cost_estimate=cost(LAYERS),
        name="layers_forward",
    )(h, seg_col, seg_row, weights)


def run_backward(upstream, states, weights, need_up):
    h_all, n_all, q_all, k_all, v_all, p_all = states
    return pl.pallas_call(
        functools.partial(backward_kernel, need_up),
        out_shape=(
            jax.ShapeDtypeStruct((LENGTH, WIDTH), BF16),
            jax.ShapeDtypeStruct((LAYERS, LENGTH, 2 * HEAD), BF16),
        ),
        in_specs=[VM] * 6 + [ANY],
        out_specs=(VM, VM),
        scratch_shapes=[WEIGHT_SCRATCH, pltpu.VMEM((LENGTH, WIDTH), F32), WEIGHT_SEMS],
        compiler_params=pltpu.CompilerParams(vmem_limit_bytes=VMEM_LIMIT),
        cost_estimate=cost(LAYERS),
        name="layers_backward",
    )(upstream, h_all, q_all, k_all, v_all, p_all, weights)


def reorder(rows):
    split = rows.reshape(LENGTH, 4, 4, 2, 2, 64)
    return split.transpose(0, 4, 3, 2, 1, 5).reshape(LENGTH, WIDTH)


def swap(block, axis):
    return lax.ppermute(block, axis, [(0, 1), (1, 0)])


def turned(block, axis, distance):
    return lax.ppermute(block, axis, [(i, (i + distance) % 4) for i in range(4)])


def pick(block, index, size, axis):
    return lax.dynamic_slice_in_dim(block, index * size, size, axis)


def to_layer(block):
    me = lax.axis_index("x")
    parts = [pick(block, me, 1, 0)]
    for distance in range(1, 4):
        parts.append(turned(pick(block, (me + distance) % 4, 1, 0), "x", distance))
    return jnp.concatenate(parts, axis=0)


def shards(
    inputs, out_grad, doc_ids, query_weight, out_weight, master, first_moment, second_moment
):
    yh, x = lax.axis_index("yh"), lax.axis_index("x")
    z1, z2, yl, c = (lax.axis_index(name) for name in DP)
    own = jnp.concatenate(
        [
            query_weight[0],
            master[0, 0].astype(BF16),
            master[0, 1].astype(BF16),
            out_weight[0],
        ],
        axis=1,
    )
    with jax.named_scope("gather_weights"):
        own = lax.all_gather(own, "x", axis=0)
        weights = lax.all_gather(own, DP, axis=0)
        weights = weights.reshape(4, 4, 2, 2, LAYERS, 64, COLS)

    rows_in = reorder(lax.dynamic_index_in_dim(inputs, x, 0, keepdims=False))
    up_in = reorder(lax.dynamic_index_in_dim(out_grad, x, 0, keepdims=False))
    segment = lax.dynamic_index_in_dim(doc_ids, x, 0, keepdims=False)
    seg_col, seg_row = segment[:, None], segment[None, :]

    first_half = run_forward(rows_in, seg_col, seg_row, weights)[0]
    arrived = swap(first_half, "yh")
    layer_in = jnp.where(yh == 1, arrived, rows_in)
    states = run_forward(layer_in, seg_col, seg_row, weights)[1:]

    half_up = run_backward(up_in, states, weights, True)[0]
    arrived = swap(half_up, "yh")
    upstream = jnp.where(yh == 0, arrived, up_in)
    grads = run_backward(upstream, states, weights, False)[1]

    with jax.named_scope("normed_slices"):
        rows = to_layer(states[1]).reshape(1, 4 * LENGTH, WIDTH)
        half = WIDTH // 2
        rows = jnp.concatenate(
            [pick(rows, c, half, 2), swap(pick(rows, 1 - c, half, 2), "c")], axis=0
        )
        half = half // 2
        rows = jnp.concatenate(
            [pick(rows, yl, half, 2), swap(pick(rows, 1 - yl, half, 2), "yl")], axis=0
        )
        quarter = half // 4
        parts = [pick(rows, z2, quarter, 2)]
        for distance in range(1, 4):
            parts.append(turned(pick(rows, (z2 + distance) % 4, quarter, 2), "z2", distance))
        rows = jnp.concatenate(parts, axis=0).reshape(-1, quarter)

    with jax.named_scope("gather_grads"):
        cols = to_layer(grads).reshape(1, 4 * LENGTH, 2 * HEAD)
        cols = jnp.concatenate([cols, swap(cols, "c")], axis=0)
        cols = jnp.concatenate([cols, swap(cols, "yl")], axis=0)
        parts = [cols] + [turned(cols, "z2", distance) for distance in range(1, 4)]
        cols = jnp.concatenate(parts, axis=0).reshape(-1, 2 * HEAD)

    with jax.named_scope("sum_grads"):
        partial = dot_tn(rows, cols)
        grad = pick(partial, z1, 64, 0)
        for distance in range(1, 4):
            grad = grad + turned(pick(partial, (z1 + distance) % 4, 64, 0), "z1", distance)
        grad = jnp.stack([grad[:, :HEAD], grad[:, HEAD:]])

    with jax.named_scope("clip"):
        total_sq = jnp.full((8, 128), jnp.sum(grad * grad))
        for axes in (("yl", "c"), "x", "z2", "z1", "yh"):
            total_sq = jnp.sum(lax.all_gather(total_sq, axes, axis=0), axis=0)
        factor = jnp.minimum(1.0, CLIP_NORM / jnp.sqrt(total_sq[0, 0]))
    clipped = grad * factor
    first_new = BETA_FIRST * first_moment[0] + (1.0 - BETA_FIRST) * clipped
    second_new = BETA_SECOND * second_moment[0] + (1.0 - BETA_SECOND) * clipped * clipped
    adam_step = first_new / (jnp.sqrt(second_new) + ADAM_EPSILON)
    fresh_shard = (master[0] - LEARN_RATE * adam_step).astype(BF16)
    return (adam_step[None], fresh_shard[None])


def solution(mesh):
    fine = Mesh(mesh.devices.reshape(tuple(FINE.values())), tuple(FINE))
    section = ("yh", "x")
    placed = (
        P(None, DP, None),
        P(None, DP, None),
        P(None, DP),
        P(section, DP, None),
        P(section, DP, None),
        P(section, None, DP, None),
        P(section, None, DP, None),
        P(section, None, DP, None),
    )
    return jax.shard_map(
        shards,
        mesh=fine,
        in_specs=placed,
        out_specs=(P(section, None, DP, None), P(section, None, DP, None)),
        check_vma=False,
    )
```

```python
import functools
import math

import jax
import jax.numpy as jnp
from jax import lax
from jax.experimental import pallas as pl
from jax.experimental.pallas import tpu as pltpu
from jax.sharding import Mesh, PartitionSpec as P

NORM_EPS = 1e-05
BETA_FIRST = 0.9
BETA_SECOND = 0.95
ADAM_EPSILON = 1e-08
LEARN_RATE = 0.001
CLIP_NORM = 1.0

FINE = {"yh": 2, "x": 4, "z": 16, "yl": 2, "c": 2}
DP = ("z", "yl", "c")
PLANE = ("x", "yl", "c")
LAYERS = 4
LENGTH = 32
WIDTH = 4096
HEAD = 128
HEADS = 4
QW = HEAD * HEADS
KVW = QW + 2 * HEAD
COLS = KVW + QW
CHUNK = 1024
SCALE = 1.0 / math.sqrt(HEAD)
VMEM_LIMIT = 60 * 1024 * 1024
F32 = jnp.float32
BF16 = jnp.bfloat16


def dot_nn(a, b):
    return lax.dot_general(a, b, (((1,), (0,)), ((), ())), preferred_element_type=F32)


def dot_nt(a, b):
    return lax.dot_general(a, b, (((1,), (1,)), ((), ())), preferred_element_type=F32)


def dot_tn(a, b):
    return lax.dot_general(a, b, (((0,), (0,)), ((), ())), preferred_element_type=F32)


def weight_copies(w_hbm, w_vmem, sems, layer):
    copies = []
    for c in range(2):
        for yl in range(2):
            at = c * 2 + yl
            copies.append(
                pltpu.make_async_copy(
                    w_hbm.at[:, yl, c, layer], w_vmem.at[layer, at], sems.at[layer, at]
                )
            )
    return copies


def stack_heads(rows):
    return jnp.concatenate([rows[:, h * HEAD : (h + 1) * HEAD] for h in range(HEADS)], axis=0)


def unstack_heads(rows):
    return jnp.concatenate([rows[h * LENGTH : (h + 1) * LENGTH] for h in range(HEADS)], axis=1)


def inverse_norm(h_ref, layer):
    total = jnp.zeros((LENGTH, 1), F32)
    for at in range(0, WIDTH, CHUNK):
        signal = h_ref[layer, :, at : at + CHUNK].astype(F32)
        total = total + jnp.sum(signal * signal, axis=-1, keepdims=True)
    return lax.rsqrt(total * (1.0 / WIDTH) + NORM_EPS)


def weight_rows(w_vmem, layer, at, first, last):
    return w_vmem[layer, at // CHUNK, :, :, first:last].reshape(CHUNK, last - first)


def forward_kernel(
    h_ref, seg_col, seg_row, w_hbm, out_ref, h_all, n_all, q_all, k_all, v_all, p_all, w_vmem, sems
):
    for layer in range(LAYERS):
        for copy in weight_copies(w_hbm, w_vmem, sems, layer):
            copy.start()
    row_ids = lax.broadcasted_iota(jnp.int32, (LENGTH, LENGTH), 0)
    col_ids = lax.broadcasted_iota(jnp.int32, (LENGTH, LENGTH), 1)
    allowed = ((seg_col[...] == seg_row[...]) & (col_ids <= row_ids)).astype(F32)
    mask = jnp.concatenate([allowed] * HEADS, axis=0) > 0.0
    h_all[0] = h_ref[...]
    for layer in range(LAYERS):
        inverse = inverse_norm(h_all, layer)
        for at in range(0, WIDTH, CHUNK):
            signal = h_all[layer, :, at : at + CHUNK].astype(F32)
            n_all[layer, :, at : at + CHUNK] = (signal * inverse).astype(BF16)
        copies = weight_copies(w_hbm, w_vmem, sems, layer)
        acc = jnp.zeros((LENGTH, KVW), F32)
        for at in range(0, WIDTH, CHUNK):
            copies[at // CHUNK].wait()
            acc = acc + dot_nn(
                n_all[layer, :, at : at + CHUNK], weight_rows(w_vmem, layer, at, 0, KVW)
            )
        rows = acc.astype(BF16)
        query = stack_heads(rows[:, :QW])
        keys = rows[:, QW : QW + HEAD]
        values = rows[:, QW + HEAD :]
        scores = dot_nt(query, keys) * SCALE
        exp_scores = jnp.where(mask, jnp.exp(scores), 0.0)
        probs = exp_scores / jnp.sum(exp_scores, axis=-1, keepdims=True)
        context = unstack_heads(dot_nn(probs.astype(BF16), values).astype(BF16))
        q_all[layer] = query
        k_all[layer] = keys
        v_all[layer] = values
        p_all[layer] = probs
        for at in range(0, WIDTH, CHUNK):
            signal = h_all[layer, :, at : at + CHUNK].astype(F32)
            branch = dot_nt(context, weight_rows(w_vmem, layer, at, KVW, COLS))
            result = (signal + branch).astype(BF16)
            if layer + 1 < LAYERS:
                h_all[layer + 1, :, at : at + CHUNK] = result
            else:
                out_ref[:, at : at + CHUNK] = result


def backward_kernel(
    need_up, up_ref, h_all, q_all, k_all, v_all, p_all, w_hbm, out_ref, g_all, w_vmem, gn, sems
):
    for layer in reversed(range(LAYERS)):
        for copy in weight_copies(w_hbm, w_vmem, sems, layer):
            copy.start()
    out_ref[...] = up_ref[...]
    for layer in reversed(range(LAYERS)):
        copies = weight_copies(w_hbm, w_vmem, sems, layer)
        acc = jnp.zeros((LENGTH, QW), F32)
        for at in range(0, WIDTH, CHUNK):
            copies[at // CHUNK].wait()
            acc = acc + dot_nn(
                out_ref[:, at : at + CHUNK], weight_rows(w_vmem, layer, at, KVW, COLS)
            )
        grad_context = stack_heads(acc.astype(BF16))
        query, keys, values, probs = q_all[layer], k_all[layer], v_all[layer], p_all[layer]
        grad_probs = dot_nt(grad_context, values)
        grad_values = dot_tn(probs.astype(BF16), grad_context).astype(BF16)
        centred = grad_probs - jnp.sum(probs * grad_probs, axis=-1, keepdims=True)
        grad_scores = (probs * centred * SCALE).astype(BF16)
        grad_query = unstack_heads(dot_nn(grad_scores, keys).astype(BF16))
        grad_keys = dot_tn(grad_scores, query).astype(BF16)
        g_all[layer, :, :HEAD] = grad_keys
        g_all[layer, :, HEAD:] = grad_values
        if layer == 0 and not need_up:
            continue
        grads = jnp.concatenate([grad_query, grad_keys, grad_values], axis=1)
        inverse = inverse_norm(h_all, layer)
        total = jnp.zeros((LENGTH, 1), F32)
        for at in range(0, WIDTH, CHUNK):
            part = dot_nt(grads, weight_rows(w_vmem, layer, at, 0, KVW))
            gn[:, at : at + CHUNK] = part
            signal = h_all[layer, :, at : at + CHUNK].astype(F32)
            total = total + jnp.sum(part * signal, axis=-1, keepdims=True)
        pull = inverse * inverse * inverse * (total * (1.0 / WIDTH))
        for at in range(0, WIDTH, CHUNK):
            signal = h_all[layer, :, at : at + CHUNK].astype(F32)
            upstream = out_ref[:, at : at + CHUNK].astype(F32)
            out_ref[:, at : at + CHUNK] = (
                upstream + inverse * gn[:, at : at + CHUNK] - signal * pull
            ).astype(BF16)


VM = pl.BlockSpec(memory_space=pltpu.VMEM)
ANY = pl.BlockSpec(memory_space=pl.ANY)
WEIGHT_SCRATCH = pltpu.VMEM((LAYERS, WIDTH // CHUNK, 16, 64, COLS), BF16)
WEIGHT_SEMS = pltpu.SemaphoreType.DMA((LAYERS, WIDTH // CHUNK))
STATE_SHAPES = (
    jax.ShapeDtypeStruct((LAYERS, LENGTH, WIDTH), BF16),
    jax.ShapeDtypeStruct((LAYERS, LENGTH, WIDTH), BF16),
    jax.ShapeDtypeStruct((LAYERS, LENGTH * HEADS, HEAD), BF16),
    jax.ShapeDtypeStruct((LAYERS, LENGTH, HEAD), BF16),
    jax.ShapeDtypeStruct((LAYERS, LENGTH, HEAD), BF16),
    jax.ShapeDtypeStruct((LAYERS, LENGTH * HEADS, LENGTH), F32),
)


def cost(products):
    return pl.CostEstimate(
        flops=products * 2 * LENGTH * WIDTH * COLS,
        bytes_accessed=LAYERS * WIDTH * COLS * 2,
        transcendentals=0,
    )


def run_forward(h, seg_col, seg_row, weights):
    return pl.pallas_call(
        forward_kernel,
        out_shape=(jax.ShapeDtypeStruct((LENGTH, WIDTH), BF16),) + STATE_SHAPES,
        in_specs=[VM, VM, VM, ANY],
        out_specs=(VM,) * 7,
        scratch_shapes=[WEIGHT_SCRATCH, WEIGHT_SEMS],
        compiler_params=pltpu.CompilerParams(vmem_limit_bytes=VMEM_LIMIT),
        cost_estimate=cost(LAYERS),
        name="layers_forward",
    )(h, seg_col, seg_row, weights)


def run_backward(upstream, states, weights, need_up):
    h_all, n_all, q_all, k_all, v_all, p_all = states
    return pl.pallas_call(
        functools.partial(backward_kernel, need_up),
        out_shape=(
            jax.ShapeDtypeStruct((LENGTH, WIDTH), BF16),
            jax.ShapeDtypeStruct((LAYERS, LENGTH, 2 * HEAD), BF16),
        ),
        in_specs=[VM] * 6 + [ANY],
        out_specs=(VM, VM),
        scratch_shapes=[WEIGHT_SCRATCH, pltpu.VMEM((LENGTH, WIDTH), F32), WEIGHT_SEMS],
        compiler_params=pltpu.CompilerParams(vmem_limit_bytes=VMEM_LIMIT),
        cost_estimate=cost(LAYERS),
        name="layers_backward",
    )(upstream, h_all, q_all, k_all, v_all, p_all, weights)


def reorder(rows):
    split = rows.reshape(LENGTH, 16, 2, 2, 64)
    return split.transpose(0, 3, 2, 1, 4).reshape(LENGTH, WIDTH)


def swap(block, axis):
    return lax.ppermute(block, axis, [(0, 1), (1, 0)])


def sum_over(value, axes, count):
    spread = jnp.broadcast_to(value, (count, 8, 128))
    return jnp.sum(lax.all_to_all(spread, axes, 0, 0, tiled=True), axis=0)


def shards(
    inputs, out_grad, doc_ids, query_weight, out_weight, master, first_moment, second_moment
):
    yh, x = lax.axis_index("yh"), lax.axis_index("x")
    own = jnp.concatenate(
        [
            query_weight[0],
            master[0, 0].astype(BF16),
            master[0, 1].astype(BF16),
            out_weight[0],
        ],
        axis=1,
    )
    with jax.named_scope("gather_weights"):
        own = lax.all_gather(own, "x", axis=0)
        weights = lax.all_gather(own, DP, axis=0)
        weights = weights.reshape(16, 2, 2, LAYERS, 64, COLS)

    rows_in = reorder(lax.dynamic_index_in_dim(inputs, x, 0, keepdims=False))
    up_in = reorder(lax.dynamic_index_in_dim(out_grad, x, 0, keepdims=False))
    segment = lax.dynamic_index_in_dim(doc_ids, x, 0, keepdims=False)
    seg_col, seg_row = segment[:, None], segment[None, :]

    first_half = run_forward(rows_in, seg_col, seg_row, weights)[0]
    arrived = swap(first_half, "yh")
    layer_in = jnp.where(yh == 1, arrived, rows_in)
    states = run_forward(layer_in, seg_col, seg_row, weights)[1:]

    half_up = run_backward(up_in, states, weights, True)[0]
    with jax.named_scope("normed_slices"):
        half_up, rows = lax.optimization_barrier((half_up, states[1]))
        arrived = swap(half_up, "yh")
        rows = rows.reshape(LAYERS, LENGTH, 2, 2, CHUNK).transpose(0, 3, 2, 1, 4)
        rows = rows.reshape(4 * LAYERS, LENGTH, CHUNK)
        rows = lax.all_to_all(rows, PLANE, 0, 0, tiled=True).reshape(-1, CHUNK)
        arrived, rows = lax.optimization_barrier((arrived, rows))
    upstream = jnp.where(yh == 0, arrived, up_in)
    grads = run_backward(upstream, states, weights, False)[1]

    with jax.named_scope("gather_grads"):
        cols = jnp.broadcast_to(grads[:, None], (LAYERS, 4, LENGTH, 2 * HEAD))
        cols = cols.reshape(4 * LAYERS, LENGTH, 2 * HEAD)
        cols = lax.all_to_all(cols, PLANE, 0, 0, tiled=True).reshape(-1, 2 * HEAD)

    with jax.named_scope("sum_grads"):
        partial = dot_tn(rows, cols).astype(BF16).reshape(16, 64, 2 * HEAD)
        parts = lax.all_to_all(partial, "z", 0, 0, tiled=True)
        grad = jnp.sum(parts.astype(F32), axis=0)
        grad = jnp.stack([grad[:, :HEAD], grad[:, HEAD:]])

    with jax.named_scope("clip"):
        total_sq = sum_over(jnp.sum(grad * grad), "z", 16)
        total_sq = sum_over(total_sq, ("yh",) + PLANE, 32)
        factor = jnp.minimum(1.0, CLIP_NORM / jnp.sqrt(total_sq[0, 0]))
    clipped = grad * factor
    first_new = BETA_FIRST * first_moment[0] + (1.0 - BETA_FIRST) * clipped
    second_new = BETA_SECOND * second_moment[0] + (1.0 - BETA_SECOND) * clipped * clipped
    adam_step = first_new / (jnp.sqrt(second_new) + ADAM_EPSILON)
    fresh_shard = (master[0] - LEARN_RATE * adam_step).astype(BF16)
    return (adam_step[None], fresh_shard[None])


def solution(mesh):
    fine = Mesh(mesh.devices.reshape(tuple(FINE.values())), tuple(FINE))
    section = ("yh", "x")
    placed = (
        P(None, DP, None),
        P(None, DP, None),
        P(None, DP),
        P(section, DP, None),
        P(section, DP, None),
        P(section, None, DP, None),
        P(section, None, DP, None),
        P(section, None, DP, None),
    )
    return jax.shard_map(
        shards,
        mesh=fine,
        in_specs=placed,
        out_specs=(P(section, None, DP, None), P(section, None, DP, None)),
        check_vma=False,
    )
```

```python
import functools
import math

import jax
import jax.numpy as jnp
from jax import lax
from jax.experimental import pallas as pl
from jax.experimental.pallas import tpu as pltpu
from jax.sharding import Mesh, PartitionSpec as P

NORM_EPS = 1e-05
BETA_FIRST = 0.9
BETA_SECOND = 0.95
ADAM_EPSILON = 1e-08
LEARN_RATE = 0.001
CLIP_NORM = 1.0

FINE = {"yh": 2, "x": 4, "z": 16, "yl": 2, "c": 2}
DP = ("z", "yl", "c")
PLANE = ("x", "yl", "c")
LAYERS = 4
LENGTH = 32
WIDTH = 4096
HEAD = 128
HEADS = 4
QW = HEAD * HEADS
KVW = QW + 2 * HEAD
COLS = KVW + QW
CHUNK = 1024
UPPER = 32
SOURCES = 10
SCALE = 1.0 / math.sqrt(HEAD)
VMEM_LIMIT = 60 * 1024 * 1024
F32 = jnp.float32
BF16 = jnp.bfloat16


def dot_nn(a, b):
    return lax.dot_general(a, b, (((1,), (0,)), ((), ())), preferred_element_type=F32)


def dot_nt(a, b):
    return lax.dot_general(a, b, (((1,), (1,)), ((), ())), preferred_element_type=F32)


def dot_tn(a, b):
    return lax.dot_general(a, b, (((0,), (0,)), ((), ())), preferred_element_type=F32)


def start_copies(at, layer, distance, core, sources, w_vmem, sems):
    whole, rest, *moved = sources

    def start(source, target):
        pltpu.make_async_copy(source, target, sems.at[layer, at]).start()

    c, yl = at // 2, at % 2
    target = w_vmem.at[layer, at]
    if distance == 0:
        start(whole.at[:, c, yl], target)
        return
    start(rest.at[:, c, distance - 1, yl], target.at[:, UPPER:])
    upper = target.at[:, :UPPER]
    for own in range(2):
        near, far, twice, back = moved[own::2]

        @pl.when((core == c) == (own == 0))
        def _(near=near, far=far, twice=twice, back=back):
            if distance == 1:
                start(near.at[:, yl], upper)
            elif distance == 3:
                start(far.at[:, yl], upper)
            else:
                start(twice.at[:, yl], upper.at[:8])
                start(back.at[:, yl], upper.at[8:])


def start_layers(order, place, sources, w_vmem, sems):
    x, core = place[0], place[1]
    for layer in order:
        for distance in range(4):

            @pl.when(((x - layer + 4) & 3) == distance)
            def _(layer=layer, distance=distance):
                for at in range(WIDTH // CHUNK):
                    start_copies(at, layer, distance, core, sources, w_vmem, sems)


def wait_rows(w_vmem, sems, layer, at):
    block = w_vmem.at[layer, at // CHUNK]
    pltpu.make_async_copy(block, block, sems.at[layer, at // CHUNK]).wait()


def stack_heads(rows):
    return jnp.concatenate([rows[:, h * HEAD : (h + 1) * HEAD] for h in range(HEADS)], axis=0)


def unstack_heads(rows):
    return jnp.concatenate([rows[h * LENGTH : (h + 1) * LENGTH] for h in range(HEADS)], axis=1)


def inverse_norm(h_ref, layer):
    total = jnp.zeros((LENGTH, 1), F32)
    for at in range(0, WIDTH, CHUNK):
        signal = h_ref[layer, :, at : at + CHUNK].astype(F32)
        total = total + jnp.sum(signal * signal, axis=-1, keepdims=True)
    return lax.rsqrt(total * (1.0 / WIDTH) + NORM_EPS)


def weight_rows(w_vmem, layer, at, first, last):
    return w_vmem[layer, at // CHUNK, :, :, first:last].reshape(CHUNK, last - first)


def forward_kernel(place, h_ref, seg_col, seg_row, *refs):
    sources, refs = refs[:SOURCES], refs[SOURCES:]
    out_ref, h_all, n_all, q_all, k_all, v_all, p_all, w_vmem, sems = refs
    start_layers(range(LAYERS), place, sources, w_vmem, sems)
    row_ids = lax.broadcasted_iota(jnp.int32, (LENGTH, LENGTH), 0)
    col_ids = lax.broadcasted_iota(jnp.int32, (LENGTH, LENGTH), 1)
    allowed = ((seg_col[...] == seg_row[...]) & (col_ids <= row_ids)).astype(F32)
    mask = jnp.concatenate([allowed] * HEADS, axis=0) > 0.0
    h_all[0] = h_ref[...]
    for layer in range(LAYERS):
        inverse = inverse_norm(h_all, layer)
        for at in range(0, WIDTH, CHUNK):
            signal = h_all[layer, :, at : at + CHUNK].astype(F32)
            n_all[layer, :, at : at + CHUNK] = (signal * inverse).astype(BF16)
        acc = jnp.zeros((LENGTH, KVW), F32)
        for at in range(0, WIDTH, CHUNK):
            wait_rows(w_vmem, sems, layer, at)
            acc = acc + dot_nn(
                n_all[layer, :, at : at + CHUNK], weight_rows(w_vmem, layer, at, 0, KVW)
            )
        rows = acc.astype(BF16)
        query = stack_heads(rows[:, :QW])
        keys = rows[:, QW : QW + HEAD]
        values = rows[:, QW + HEAD :]
        scores = dot_nt(query, keys) * SCALE
        exp_scores = jnp.where(mask, jnp.exp(scores), 0.0)
        probs = exp_scores / jnp.sum(exp_scores, axis=-1, keepdims=True)
        context = unstack_heads(dot_nn(probs.astype(BF16), values).astype(BF16))
        q_all[layer] = query
        k_all[layer] = keys
        v_all[layer] = values
        p_all[layer] = probs
        for at in range(0, WIDTH, CHUNK):
            signal = h_all[layer, :, at : at + CHUNK].astype(F32)
            branch = dot_nt(context, weight_rows(w_vmem, layer, at, KVW, COLS))
            result = (signal + branch).astype(BF16)
            if layer + 1 < LAYERS:
                h_all[layer + 1, :, at : at + CHUNK] = result
            else:
                out_ref[:, at : at + CHUNK] = result


def backward_kernel(need_up, place, up_ref, h_all, q_all, k_all, v_all, p_all, *refs):
    sources, refs = refs[:SOURCES], refs[SOURCES:]
    out_ref, g_all, w_vmem, gn, sems = refs
    start_layers(reversed(range(LAYERS)), place, sources, w_vmem, sems)
    out_ref[...] = up_ref[...]
    for layer in reversed(range(LAYERS)):
        acc = jnp.zeros((LENGTH, QW), F32)
        for at in range(0, WIDTH, CHUNK):
            wait_rows(w_vmem, sems, layer, at)
            acc = acc + dot_nn(
                out_ref[:, at : at + CHUNK], weight_rows(w_vmem, layer, at, KVW, COLS)
            )
        grad_context = stack_heads(acc.astype(BF16))
        query, keys, values, probs = q_all[layer], k_all[layer], v_all[layer], p_all[layer]
        grad_probs = dot_nt(grad_context, values)
        grad_values = dot_tn(probs.astype(BF16), grad_context).astype(BF16)
        centred = grad_probs - jnp.sum(probs * grad_probs, axis=-1, keepdims=True)
        grad_scores = (probs * centred * SCALE).astype(BF16)
        grad_query = unstack_heads(dot_nn(grad_scores, keys).astype(BF16))
        grad_keys = dot_tn(grad_scores, query).astype(BF16)
        g_all[layer, :, :HEAD] = grad_keys
        g_all[layer, :, HEAD:] = grad_values
        if layer == 0 and not need_up:
            continue
        grads = jnp.concatenate([grad_query, grad_keys, grad_values], axis=1)
        inverse = inverse_norm(h_all, layer)
        total = jnp.zeros((LENGTH, 1), F32)
        for at in range(0, WIDTH, CHUNK):
            part = dot_nt(grads, weight_rows(w_vmem, layer, at, 0, KVW))
            gn[:, at : at + CHUNK] = part
            signal = h_all[layer, :, at : at + CHUNK].astype(F32)
            total = total + jnp.sum(part * signal, axis=-1, keepdims=True)
        pull = inverse * inverse * inverse * (total * (1.0 / WIDTH))
        for at in range(0, WIDTH, CHUNK):
            signal = h_all[layer, :, at : at + CHUNK].astype(F32)
            upstream = out_ref[:, at : at + CHUNK].astype(F32)
            out_ref[:, at : at + CHUNK] = (
                upstream + inverse * gn[:, at : at + CHUNK] - signal * pull
            ).astype(BF16)


VM = pl.BlockSpec(memory_space=pltpu.VMEM)
SM = pl.BlockSpec(memory_space=pltpu.SMEM)
ANY = pl.BlockSpec(memory_space=pl.ANY)
WEIGHT_SCRATCH = pltpu.VMEM((LAYERS, WIDTH // CHUNK, 16, 64, COLS), BF16)
WEIGHT_SEMS = pltpu.SemaphoreType.DMA((LAYERS, WIDTH // CHUNK))
STATE_SHAPES = (
    jax.ShapeDtypeStruct((LAYERS, LENGTH, WIDTH), BF16),
    jax.ShapeDtypeStruct((LAYERS, LENGTH, WIDTH), BF16),
    jax.ShapeDtypeStruct((LAYERS, LENGTH * HEADS, HEAD), BF16),
    jax.ShapeDtypeStruct((LAYERS, LENGTH, HEAD), BF16),
    jax.ShapeDtypeStruct((LAYERS, LENGTH, HEAD), BF16),
    jax.ShapeDtypeStruct((LAYERS, LENGTH * HEADS, LENGTH), F32),
)


def cost(products):
    return pl.CostEstimate(
        flops=products * 2 * LENGTH * WIDTH * COLS,
        bytes_accessed=LAYERS * WIDTH * COLS * 2,
        transcendentals=0,
    )


def run_forward(place, h, seg_col, seg_row, weights):
    return pl.pallas_call(
        forward_kernel,
        out_shape=(jax.ShapeDtypeStruct((LENGTH, WIDTH), BF16),) + STATE_SHAPES,
        in_specs=[SM, VM, VM, VM] + [ANY] * SOURCES,
        out_specs=(VM,) * 7,
        scratch_shapes=[WEIGHT_SCRATCH, WEIGHT_SEMS],
        compiler_params=pltpu.CompilerParams(vmem_limit_bytes=VMEM_LIMIT),
        cost_estimate=cost(LAYERS),
        name="layers_forward",
    )(place, h, seg_col, seg_row, *weights)


def run_backward(place, upstream, states, weights, need_up):
    h_all, n_all, q_all, k_all, v_all, p_all = states
    return pl.pallas_call(
        functools.partial(backward_kernel, need_up),
        out_shape=(
            jax.ShapeDtypeStruct((LENGTH, WIDTH), BF16),
            jax.ShapeDtypeStruct((LAYERS, LENGTH, 2 * HEAD), BF16),
        ),
        in_specs=[SM] + [VM] * 6 + [ANY] * SOURCES,
        out_specs=(VM, VM),
        scratch_shapes=[WEIGHT_SCRATCH, pltpu.VMEM((LENGTH, WIDTH), F32), WEIGHT_SEMS],
        compiler_params=pltpu.CompilerParams(vmem_limit_bytes=VMEM_LIMIT),
        cost_estimate=cost(LAYERS),
        name="layers_backward",
    )(place, upstream, h_all, q_all, k_all, v_all, p_all, *weights)


def reorder(rows):
    split = rows.reshape(LENGTH, 16, 2, 2, 64)
    return split.transpose(0, 3, 2, 1, 4).reshape(LENGTH, WIDTH)


def swap(block, axis):
    return lax.ppermute(block, axis, [(0, 1), (1, 0)])


def turned(block, distance):
    return lax.ppermute(block, "x", [(i, (i + distance) % 4) for i in range(4)])


def gather_layers(own, yl, c):
    other = swap(own, "yl")
    pair = jnp.stack([jnp.where(yl == 0, own, other), jnp.where(yl == 0, other, own)])
    whole = lax.all_gather(pair, ("z", "c"), axis=0).reshape(16, 2, 2, 64, COLS)
    lower = pair[:, UPPER:]
    lower = jnp.stack([turned(lower, distance) for distance in range(1, 4)])
    rest = lax.all_gather(lower, ("z", "c"), axis=0).reshape(16, 2, 3, 2, 64 - UPPER, COLS)
    share = lax.dynamic_slice(whole, (0, c, 0, 0, 0), (16, 1, 2, UPPER, COLS))[:, 0]
    near, far = turned(share, 1), turned(share, 3)
    twice, back = turned(near[:8], 1), turned(far[8:], 3)
    moved = []
    for block in (near, far, twice, back):
        moved += [block, swap(block, "c")]
    return [whole, rest] + moved


def sum_over(value, axes, count):
    spread = jnp.broadcast_to(value, (count, 8, 128))
    return jnp.sum(lax.all_to_all(spread, axes, 0, 0, tiled=True), axis=0)


def shards(
    inputs, out_grad, doc_ids, query_weight, out_weight, master, first_moment, second_moment
):
    yh, x = lax.axis_index("yh"), lax.axis_index("x")
    own = jnp.concatenate(
        [
            query_weight[0],
            master[0, 0].astype(BF16),
            master[0, 1].astype(BF16),
            out_weight[0],
        ],
        axis=1,
    )
    with jax.named_scope("gather_weights"):
        weights = gather_layers(own, lax.axis_index("yl"), lax.axis_index("c"))
    place = jnp.stack([x, lax.axis_index("c")]).astype(jnp.int32)

    rows_in = reorder(lax.dynamic_index_in_dim(inputs, x, 0, keepdims=False))
    up_in = reorder(lax.dynamic_index_in_dim(out_grad, x, 0, keepdims=False))
    segment = lax.dynamic_index_in_dim(doc_ids, x, 0, keepdims=False)
    seg_col, seg_row = segment[:, None], segment[None, :]

    first_half = run_forward(place, rows_in, seg_col, seg_row, weights)[0]
    arrived = swap(first_half, "yh")
    layer_in = jnp.where(yh == 1, arrived, rows_in)
    states = run_forward(place, layer_in, seg_col, seg_row, weights)[1:]

    half_up = run_backward(place, up_in, states, weights, True)[0]
    with jax.named_scope("normed_slices"):
        rows = states[1].reshape(LAYERS, LENGTH, 2, 2, CHUNK).transpose(0, 3, 2, 1, 4)
        rows = rows.reshape(4 * LAYERS, LENGTH, CHUNK)
        rows = lax.all_to_all(rows, PLANE, 0, 0, tiled=True).reshape(-1, CHUNK)
        half_up, rows = lax.optimization_barrier((half_up, rows))
    arrived = swap(half_up, "yh")
    upstream = jnp.where(yh == 0, arrived, up_in)
    grads = run_backward(place, upstream, states, weights, False)[1]

    with jax.named_scope("gather_grads"):
        cols = jnp.broadcast_to(grads[:, None], (LAYERS, 4, LENGTH, 2 * HEAD))
        cols = cols.reshape(4 * LAYERS, LENGTH, 2 * HEAD)
        cols = lax.all_to_all(cols, PLANE, 0, 0, tiled=True).reshape(-1, 2 * HEAD)

    with jax.named_scope("sum_grads"):
        partial = dot_tn(rows, cols).astype(BF16).reshape(16, 64, 2 * HEAD)
        parts = lax.all_to_all(partial, "z", 0, 0, tiled=True)
        grad = jnp.sum(parts.astype(F32), axis=0)
        grad = jnp.stack([grad[:, :HEAD], grad[:, HEAD:]])

    with jax.named_scope("clip"):
        total_sq = sum_over(jnp.sum(grad * grad), "z", 16)
        total_sq = sum_over(total_sq, ("yh",) + PLANE, 32)
        factor = jnp.minimum(1.0, CLIP_NORM / jnp.sqrt(total_sq[0, 0]))
    clipped = grad * factor
    first_new = BETA_FIRST * first_moment[0] + (1.0 - BETA_FIRST) * clipped
    second_new = BETA_SECOND * second_moment[0] + (1.0 - BETA_SECOND) * clipped * clipped
    adam_step = first_new / (jnp.sqrt(second_new) + ADAM_EPSILON)
    fresh_shard = (master[0] - LEARN_RATE * adam_step).astype(BF16)
    return (adam_step[None], fresh_shard[None])


def solution(mesh):
    fine = Mesh(mesh.devices.reshape(tuple(FINE.values())), tuple(FINE))
    section = ("yh", "x")
    placed = (
        P(None, DP, None),
        P(None, DP, None),
        P(None, DP),
        P(section, DP, None),
        P(section, DP, None),
        P(section, None, DP, None),
        P(section, None, DP, None),
        P(section, None, DP, None),
    )
    return jax.shard_map(
        shards,
        mesh=fine,
        in_specs=placed,
        out_specs=(P(section, None, DP, None), P(section, None, DP, None)),
        check_vma=False,
    )
```

```python
import functools
import math

import jax
import jax.numpy as jnp
from jax import lax
from jax.experimental import pallas as pl
from jax.experimental.pallas import tpu as pltpu
from jax.sharding import Mesh, PartitionSpec as P

NORM_EPS = 1e-05
BETA_FIRST = 0.9
BETA_SECOND = 0.95
ADAM_EPSILON = 1e-08
LEARN_RATE = 0.001
CLIP_NORM = 1.0

FINE = {"yh": 2, "x": 4, "z": 16, "yl": 2, "c": 2}
DP = ("z", "yl", "c")
PLANE = ("x", "yl", "c")
LAYERS = 4
LENGTH = 32
WIDTH = 4096
HEAD = 128
HEADS = 4
QW = HEAD * HEADS
KVW = QW + 2 * HEAD
COLS = KVW + QW
CHUNK = 1024
UPPER = 32
SOURCES = 14
SCALE = 1.0 / math.sqrt(HEAD)
VMEM_LIMIT = 60 * 1024 * 1024
F32 = jnp.float32
BF16 = jnp.bfloat16


def dot_nn(a, b):
    return lax.dot_general(a, b, (((1,), (0,)), ((), ())), preferred_element_type=F32)


def dot_nt(a, b):
    return lax.dot_general(a, b, (((1,), (1,)), ((), ())), preferred_element_type=F32)


def dot_tn(a, b):
    return lax.dot_general(a, b, (((0,), (0,)), ((), ())), preferred_element_type=F32)


def start_copies(at, layer, distance, core, sources, w_vmem, sems):
    whole, rest, *moved = sources

    def start(source, target):
        pltpu.make_async_copy(source, target, sems.at[layer, at]).start()

    c, yl = at // 2, at % 2
    target = w_vmem.at[layer, at]
    if distance == 0:
        start(whole.at[:, c, yl], target)
        return
    start(rest.at[:, c, distance - 1, yl], target.at[:, UPPER:])
    upper = target.at[:, :UPPER]
    for own in range(2):

        @pl.when((core == c) == (own == 0))
        def _(own=own):
            for half in range(2):
                block = moved[(distance - 1) * 4 + half * 2 + own]
                start(block.at[:, yl], upper.at[half * 8 : half * 8 + 8])


def start_layers(order, place, sources, w_vmem, sems):
    x, core = place[0], place[1]
    for layer in order:
        for distance in range(4):

            @pl.when(((x - layer + 4) & 3) == distance)
            def _(layer=layer, distance=distance):
                for at in range(WIDTH // CHUNK):
                    start_copies(at, layer, distance, core, sources, w_vmem, sems)


def wait_rows(w_vmem, sems, layer, at):
    block = w_vmem.at[layer, at // CHUNK]
    pltpu.make_async_copy(block, block, sems.at[layer, at // CHUNK]).wait()


def stack_heads(rows):
    return jnp.concatenate([rows[:, h * HEAD : (h + 1) * HEAD] for h in range(HEADS)], axis=0)


def unstack_heads(rows):
    return jnp.concatenate([rows[h * LENGTH : (h + 1) * LENGTH] for h in range(HEADS)], axis=1)


def inverse_norm(h_ref, layer):
    total = jnp.zeros((LENGTH, 1), F32)
    for at in range(0, WIDTH, CHUNK):
        signal = h_ref[layer, :, at : at + CHUNK].astype(F32)
        total = total + jnp.sum(signal * signal, axis=-1, keepdims=True)
    return lax.rsqrt(total * (1.0 / WIDTH) + NORM_EPS)


def weight_rows(w_vmem, layer, at, first, last):
    return w_vmem[layer, at // CHUNK, :, :, first:last].reshape(CHUNK, last - first)


def attention_mask(seg_col, seg_row):
    row_ids = lax.broadcasted_iota(jnp.int32, (LENGTH, LENGTH), 0)
    col_ids = lax.broadcasted_iota(jnp.int32, (LENGTH, LENGTH), 1)
    allowed = ((seg_col[...] == seg_row[...]) & (col_ids <= row_ids)).astype(F32)
    return jnp.concatenate([allowed] * HEADS, axis=0) > 0.0


def forward_layers(mask, h_all, n_all, kept, out_ref, w_vmem, sems):
    for layer in range(LAYERS):
        inverse = inverse_norm(h_all, layer)
        for at in range(0, WIDTH, CHUNK):
            signal = h_all[layer, :, at : at + CHUNK].astype(F32)
            n_all[layer, :, at : at + CHUNK] = (signal * inverse).astype(BF16)
        acc = jnp.zeros((LENGTH, KVW), F32)
        for at in range(0, WIDTH, CHUNK):
            wait_rows(w_vmem, sems, layer, at)
            acc = acc + dot_nn(
                n_all[layer, :, at : at + CHUNK], weight_rows(w_vmem, layer, at, 0, KVW)
            )
        rows = acc.astype(BF16)
        query = stack_heads(rows[:, :QW])
        keys = rows[:, QW : QW + HEAD]
        values = rows[:, QW + HEAD :]
        scores = dot_nt(query, keys) * SCALE
        exp_scores = jnp.where(mask, jnp.exp(scores), 0.0)
        probs = exp_scores / jnp.sum(exp_scores, axis=-1, keepdims=True)
        context = unstack_heads(dot_nn(probs.astype(BF16), values).astype(BF16))
        if kept is not None:
            for ref, value in zip(kept, (query, keys, values, probs)):
                ref[layer] = value
        if out_ref is None and layer + 1 == LAYERS:
            return
        for at in range(0, WIDTH, CHUNK):
            signal = h_all[layer, :, at : at + CHUNK].astype(F32)
            branch = dot_nt(context, weight_rows(w_vmem, layer, at, KVW, COLS))
            result = (signal + branch).astype(BF16)
            if layer + 1 < LAYERS:
                h_all[layer + 1, :, at : at + CHUNK] = result
            else:
                out_ref[:, at : at + CHUNK] = result


def backward_layers(need_up, h_all, kept, up, g_all, w_vmem, gn, sems):
    q_all, k_all, v_all, p_all = kept
    for layer in reversed(range(LAYERS)):
        acc = jnp.zeros((LENGTH, QW), F32)
        for at in range(0, WIDTH, CHUNK):
            if sems is not None:
                wait_rows(w_vmem, sems, layer, at)
            acc = acc + dot_nn(up[:, at : at + CHUNK], weight_rows(w_vmem, layer, at, KVW, COLS))
        grad_context = stack_heads(acc.astype(BF16))
        query, keys, values, probs = q_all[layer], k_all[layer], v_all[layer], p_all[layer]
        grad_probs = dot_nt(grad_context, values)
        centred = grad_probs - jnp.sum(probs * grad_probs, axis=-1, keepdims=True)
        grad_scores = (probs * centred * SCALE).astype(BF16)
        grad_keys = dot_tn(grad_scores, query).astype(BF16)
        grad_values = dot_tn(probs.astype(BF16), grad_context).astype(BF16)
        if g_all is not None:
            g_all[layer, :, :HEAD] = grad_keys
            g_all[layer, :, HEAD:] = grad_values
        if layer == 0 and not need_up:
            return
        grad_query = unstack_heads(dot_nn(grad_scores, keys).astype(BF16))
        grads = jnp.concatenate([grad_query, grad_keys, grad_values], axis=1)
        inverse = inverse_norm(h_all, layer)
        total = jnp.zeros((LENGTH, 1), F32)
        for at in range(0, WIDTH, CHUNK):
            part = dot_nt(grads, weight_rows(w_vmem, layer, at, 0, KVW))
            gn[:, at : at + CHUNK] = part
            signal = h_all[layer, :, at : at + CHUNK].astype(F32)
            total = total + jnp.sum(part * signal, axis=-1, keepdims=True)
        pull = inverse * inverse * inverse * (total * (1.0 / WIDTH))
        for at in range(0, WIDTH, CHUNK):
            signal = h_all[layer, :, at : at + CHUNK].astype(F32)
            upstream = up[:, at : at + CHUNK].astype(F32)
            up[:, at : at + CHUNK] = (
                upstream + inverse * gn[:, at : at + CHUNK] - signal * pull
            ).astype(BF16)


def first_kernel(place, h_ref, seg_col, seg_row, *refs):
    sources, refs = refs[:SOURCES], refs[SOURCES:]
    out_ref, h_all, n_all, w_vmem, sems = refs
    start_layers(range(LAYERS), place, sources, w_vmem, sems)
    h_all[0] = h_ref[...]
    forward_layers(attention_mask(seg_col, seg_row), h_all, n_all, None, out_ref, w_vmem, sems)


def middle_kernel(place, h_ref, arrived, up_ref, seg_col, seg_row, *refs):
    sources, refs = refs[:SOURCES], refs[SOURCES:]
    out_ref, h_all, n_all, q_all, k_all, v_all, p_all, w_vmem, gn, sems = refs
    start_layers(range(LAYERS), place, sources, w_vmem, sems)

    @pl.when(place[2] == 1)
    def _():
        h_all[0] = arrived[...]

    @pl.when(place[2] == 0)
    def _():
        h_all[0] = h_ref[...]

    out_ref[...] = up_ref[...]
    kept = (q_all, k_all, v_all, p_all)
    forward_layers(attention_mask(seg_col, seg_row), h_all, n_all, kept, None, w_vmem, sems)
    backward_layers(True, h_all, kept, out_ref, None, w_vmem, gn, None)


def last_kernel(place, up_ref, arrived, h_all, q_all, k_all, v_all, p_all, *refs):
    sources, refs = refs[:SOURCES], refs[SOURCES:]
    g_all, up, w_vmem, gn, sems = refs
    start_layers(reversed(range(LAYERS)), place, sources, w_vmem, sems)

    @pl.when(place[2] == 0)
    def _():
        up[...] = arrived[...]

    @pl.when(place[2] == 1)
    def _():
        up[...] = up_ref[...]

    kept = (q_all, k_all, v_all, p_all)
    backward_layers(False, h_all, kept, up, g_all, w_vmem, gn, sems)


VM = pl.BlockSpec(memory_space=pltpu.VMEM)
SM = pl.BlockSpec(memory_space=pltpu.SMEM)
ANY = pl.BlockSpec(memory_space=pl.ANY)
WEIGHT_SCRATCH = pltpu.VMEM((LAYERS, WIDTH // CHUNK, 16, 64, COLS), BF16)
WEIGHT_SEMS = pltpu.SemaphoreType.DMA((LAYERS, WIDTH // CHUNK))
ROWS = jax.ShapeDtypeStruct((LENGTH, WIDTH), BF16)
ROWS_F32 = pltpu.VMEM((LENGTH, WIDTH), F32)
ROWS_ALL = pltpu.VMEM((LAYERS, LENGTH, WIDTH), BF16)
STATE_SHAPES = (
    jax.ShapeDtypeStruct((LAYERS, LENGTH, WIDTH), BF16),
    jax.ShapeDtypeStruct((LAYERS, LENGTH, WIDTH), BF16),
    jax.ShapeDtypeStruct((LAYERS, LENGTH * HEADS, HEAD), BF16),
    jax.ShapeDtypeStruct((LAYERS, LENGTH, HEAD), BF16),
    jax.ShapeDtypeStruct((LAYERS, LENGTH, HEAD), BF16),
    jax.ShapeDtypeStruct((LAYERS, LENGTH * HEADS, LENGTH), F32),
)


def cost(products):
    return pl.CostEstimate(
        flops=products * 2 * LENGTH * WIDTH * COLS,
        bytes_accessed=LAYERS * WIDTH * COLS * 2,
        transcendentals=0,
    )


def call(kernel, name, products, out_shape, inputs, sources, scratch):
    return pl.pallas_call(
        kernel,
        out_shape=out_shape,
        in_specs=[SM] + [VM] * (len(inputs) - 1) + [ANY] * SOURCES,
        out_specs=(VM,) * len(out_shape),
        scratch_shapes=scratch,
        compiler_params=pltpu.CompilerParams(vmem_limit_bytes=VMEM_LIMIT),
        cost_estimate=cost(products),
        name=name,
    )(*inputs, *sources)


def reorder(rows):
    split = rows.reshape(LENGTH, 16, 2, 2, 64)
    return split.transpose(0, 3, 2, 1, 4).reshape(LENGTH, WIDTH)


def swap(block, axis):
    return lax.ppermute(block, axis, [(0, 1), (1, 0)])


def turned(block, distance):
    return lax.ppermute(block, "x", [(i, (i + distance) % 4) for i in range(4)])


def across(block):
    return lax.ppermute(block, ("yh", "yl"), [(i, 3 - i) for i in range(4)])


def pair_rows(own, yl):
    other = swap(own, "yl")
    return jnp.stack([jnp.where(yl == 0, own, other), jnp.where(yl == 0, other, own)])


def gather_layers(pair, lower, c):
    whole = lax.all_gather(pair, ("z", "c"), axis=0).reshape(16, 2, 2, 64, COLS)
    lower = jnp.stack([turned(lower, distance) for distance in range(1, 4)])
    rest = lax.all_gather(lower, ("z", "c"), axis=0).reshape(16, 2, 3, 2, 64 - UPPER, COLS)
    share = lax.dynamic_slice(whole, (0, c, 0, 0, 0), (16, 1, 2, UPPER, COLS))[:, 0]
    low, high = share[:8], share[8:]
    near_low, far_high = turned(low, 1), turned(high, 3)
    near_low, far_high, low, high = lax.optimization_barrier((near_low, far_high, low, high))
    twice_low, twice_high = turned(near_low, 1), turned(far_high, 3)
    near_high, far_low = turned(high, 1), turned(low, 3)
    moved = []
    for block in (near_low, near_high, twice_low, twice_high, far_low, far_high):
        moved += [block, swap(block, "c")]
    return [whole, rest] + moved


def sum_over(value, axes, count):
    spread = jnp.broadcast_to(value, (count, 8, 128))
    return jnp.sum(lax.all_to_all(spread, axes, 0, 0, tiled=True), axis=0)


def shards(
    inputs, out_grad, doc_ids, query_weight, out_weight, master, first_moment, second_moment
):
    yh, x, yl, c = (lax.axis_index(name) for name in ("yh", "x", "yl", "c"))
    own = jnp.concatenate(
        [
            query_weight[0],
            master[0, 0].astype(BF16),
            master[0, 1].astype(BF16),
            out_weight[0],
        ],
        axis=1,
    )
    segment = lax.dynamic_index_in_dim(doc_ids, x, 0, keepdims=False)
    rows_in = reorder(lax.dynamic_index_in_dim(inputs, x, 0, keepdims=False))
    up_in = reorder(lax.dynamic_index_in_dim(out_grad, x, 0, keepdims=False))
    up_in = swap(up_in, "yl")
    segment = jnp.where(yh == 1, swap(segment, "yl"), segment)
    seg_col, seg_row = segment[:, None], segment[None, :]
    place = jnp.stack([x, c, yh]).astype(jnp.int32)
    with jax.named_scope("gather_weights"):
        pair = pair_rows(own, yl)
        tied = lax.optimization_barrier(
            (pair[:, UPPER:], place, rows_in, up_in, seg_col, seg_row)
        )
        lower, place, rows_in, up_in, seg_col, seg_row = tied
        sources = gather_layers(pair, lower, c)

    (arrived,) = call(
        first_kernel,
        "first_forward",
        LAYERS,
        (ROWS,),
        (place, rows_in, seg_col, seg_row),
        sources,
        [ROWS_ALL, ROWS_ALL, WEIGHT_SCRATCH, WEIGHT_SEMS],
    )
    arrived = across(arrived)
    half_up, h_all, n_all, *kept = call(
        middle_kernel,
        "second_forward_backward",
        2 * LAYERS,
        (ROWS,) + STATE_SHAPES,
        (place, rows_in, arrived, up_in, seg_col, seg_row),
        sources,
        [WEIGHT_SCRATCH, ROWS_F32, WEIGHT_SEMS],
    )
    with jax.named_scope("normed_slices"):
        rows = n_all.reshape(LAYERS, LENGTH, 2, 2, CHUNK).transpose(0, 3, 2, 1, 4)
        rows = rows.reshape(4 * LAYERS, LENGTH, CHUNK)
        rows = lax.all_to_all(rows, PLANE, 0, 0, tiled=True).reshape(-1, CHUNK)
    arrived = across(half_up)
    (grads,) = call(
        last_kernel,
        "first_backward",
        LAYERS,
        (jax.ShapeDtypeStruct((LAYERS, LENGTH, 2 * HEAD), BF16),),
        (place, up_in, arrived, h_all, *kept),
        sources,
        [pltpu.VMEM((LENGTH, WIDTH), BF16), WEIGHT_SCRATCH, ROWS_F32, WEIGHT_SEMS],
    )

    with jax.named_scope("gather_grads"):
        cols = jnp.broadcast_to(grads[:, None], (LAYERS, 4, LENGTH, 2 * HEAD))
        cols = cols.reshape(4 * LAYERS, LENGTH, 2 * HEAD)
        cols = lax.all_to_all(cols, PLANE, 0, 0, tiled=True).reshape(-1, 2 * HEAD)

    with jax.named_scope("sum_grads"):
        partial = dot_tn(rows, cols).astype(BF16).reshape(16, 64, 2 * HEAD)
        parts = lax.all_to_all(partial, "z", 0, 0, tiled=True)
        grad = jnp.sum(parts.astype(F32), axis=0)
        grad = jnp.stack([grad[:, :HEAD], grad[:, HEAD:]])

    with jax.named_scope("clip"):
        total_sq = sum_over(jnp.sum(grad * grad), "z", 16)
        total_sq = sum_over(total_sq, ("yh",) + PLANE, 32)
        factor = jnp.minimum(1.0, CLIP_NORM / jnp.sqrt(total_sq[0, 0]))
    clipped = grad * factor
    first_new = BETA_FIRST * first_moment[0] + (1.0 - BETA_FIRST) * clipped
    second_new = BETA_SECOND * second_moment[0] + (1.0 - BETA_SECOND) * clipped * clipped
    adam_step = first_new / (jnp.sqrt(second_new) + ADAM_EPSILON)
    fresh_shard = (master[0] - LEARN_RATE * adam_step).astype(BF16)
    return (adam_step[None], fresh_shard[None])


def solution(mesh):
    fine = Mesh(mesh.devices.reshape(tuple(FINE.values())), tuple(FINE))
    section = ("yh", "x")
    placed = (
        P(None, DP, None),
        P(None, DP, None),
        P(None, DP),
        P(section, DP, None),
        P(section, DP, None),
        P(section, None, DP, None),
        P(section, None, DP, None),
        P(section, None, DP, None),
    )
    return jax.shard_map(
        shards,
        mesh=fine,
        in_specs=placed,
        out_specs=(P(section, None, DP, None), P(section, None, DP, None)),
        check_vma=False,
    )
```

```python
import functools
import math

import jax
import jax.numpy as jnp
from jax import lax
from jax.experimental import pallas as pl
from jax.experimental.pallas import tpu as pltpu
from jax.sharding import Mesh, PartitionSpec as P

NORM_EPS = 1e-05
BETA_FIRST = 0.9
BETA_SECOND = 0.95
ADAM_EPSILON = 1e-08
LEARN_RATE = 0.001
CLIP_NORM = 1.0

FINE = {"yh": 2, "x": 4, "z": 16, "yl": 2, "c": 2}
DP = ("z", "yl", "c")
PLANE = ("x", "yl", "c")
LAYERS = 4
LENGTH = 32
WIDTH = 4096
HEAD = 128
HEADS = 4
QW = HEAD * HEADS
KVW = QW + 2 * HEAD
COLS = KVW + QW
CHUNK = 1024
UPPER = 48
EARLY = 8
REST_AT = {1: 0, 3: 64 - UPPER, 2: 2 * (64 - UPPER)}
SOURCES = 10
SCALE = 1.0 / math.sqrt(HEAD)
VMEM_LIMIT = 60 * 1024 * 1024
F32 = jnp.float32
BF16 = jnp.bfloat16


def dot_nn(a, b):
    return lax.dot_general(a, b, (((1,), (0,)), ((), ())), preferred_element_type=F32)


def dot_nt(a, b):
    return lax.dot_general(a, b, (((1,), (1,)), ((), ())), preferred_element_type=F32)


def dot_tn(a, b):
    return lax.dot_general(a, b, (((0,), (0,)), ((), ())), preferred_element_type=F32)


def start_copies(layer, distance, place, sources, w_vmem, sems):
    whole, rest, *moved = sources
    core, side = place[1], place[3]
    for c in range(2):
        for other in range(2):
            at = c * 2 + (side if other == 0 else 1 - side)

            def start(source, first, last, low=0, high=16, at=at):
                target = w_vmem.at[layer, at, low:high, first:last]
                pltpu.make_async_copy(source, target, sems.at[layer, at]).start()

            if distance == 0:
                start(whole.at[:, c, other], 0, 64)
                continue
            begin = REST_AT[distance]
            first = 0 if distance == 2 else UPPER
            start(rest.at[:, c, other, begin : begin + 64 - first], first, 64)
            if distance == 2:
                continue
            for own in range(2):

                @pl.when((core == c) == (own == 0))
                def _(own=own, other=other, start=start):
                    early, late = moved[(distance // 2) * 4 + own], moved[(distance // 2) * 4 + 2 + own]
                    start(early.at[:, other], 0, UPPER, 0, EARLY)
                    start(late.at[:, other], 0, UPPER, EARLY, 16)


def start_layers(order, place, sources, w_vmem, sems):
    x = place[0]
    for layer in order:
        for distance in range(4):

            @pl.when(((x - layer + 4) & 3) == distance)
            def _(layer=layer, distance=distance):
                start_copies(layer, distance, place, sources, w_vmem, sems)


def wait_rows(w_vmem, sems, layer, at):
    block = w_vmem.at[layer, at // CHUNK]
    pltpu.make_async_copy(block, block, sems.at[layer, at // CHUNK]).wait()


def stack_heads(rows):
    return jnp.concatenate([rows[:, h * HEAD : (h + 1) * HEAD] for h in range(HEADS)], axis=0)


def unstack_heads(rows):
    return jnp.concatenate([rows[h * LENGTH : (h + 1) * LENGTH] for h in range(HEADS)], axis=1)


def inverse_norm(h_ref, layer):
    total = jnp.zeros((LENGTH, 1), F32)
    for at in range(0, WIDTH, CHUNK):
        signal = h_ref[layer, :, at : at + CHUNK].astype(F32)
        total = total + jnp.sum(signal * signal, axis=-1, keepdims=True)
    return lax.rsqrt(total * (1.0 / WIDTH) + NORM_EPS)


def weight_rows(w_vmem, layer, at, first, last):
    return w_vmem[layer, at // CHUNK, :, :, first:last].reshape(CHUNK, last - first)


def attention_mask(seg_col, seg_row):
    row_ids = lax.broadcasted_iota(jnp.int32, (LENGTH, LENGTH), 0)
    col_ids = lax.broadcasted_iota(jnp.int32, (LENGTH, LENGTH), 1)
    allowed = ((seg_col[...] == seg_row[...]) & (col_ids <= row_ids)).astype(F32)
    return jnp.concatenate([allowed] * HEADS, axis=0) > 0.0


def forward_layers(mask, h_all, n_all, kept, out_ref, w_vmem, sems):
    for layer in range(LAYERS):
        inverse = inverse_norm(h_all, layer)
        for at in range(0, WIDTH, CHUNK):
            signal = h_all[layer, :, at : at + CHUNK].astype(F32)
            n_all[layer, :, at : at + CHUNK] = (signal * inverse).astype(BF16)
        acc = jnp.zeros((LENGTH, KVW), F32)
        for at in range(0, WIDTH, CHUNK):
            wait_rows(w_vmem, sems, layer, at)
            acc = acc + dot_nn(
                n_all[layer, :, at : at + CHUNK], weight_rows(w_vmem, layer, at, 0, KVW)
            )
        rows = acc.astype(BF16)
        query = stack_heads(rows[:, :QW])
        keys = rows[:, QW : QW + HEAD]
        values = rows[:, QW + HEAD :]
        scores = dot_nt(query, keys) * SCALE
        exp_scores = jnp.where(mask, jnp.exp(scores), 0.0)
        probs = exp_scores / jnp.sum(exp_scores, axis=-1, keepdims=True)
        context = unstack_heads(dot_nn(probs.astype(BF16), values).astype(BF16))
        if kept is not None:
            for ref, value in zip(kept, (query, keys, values, probs)):
                ref[layer] = value
        if out_ref is None and layer + 1 == LAYERS:
            return
        for at in range(0, WIDTH, CHUNK):
            signal = h_all[layer, :, at : at + CHUNK].astype(F32)
            branch = dot_nt(context, weight_rows(w_vmem, layer, at, KVW, COLS))
            result = (signal + branch).astype(BF16)
            if layer + 1 < LAYERS:
                h_all[layer + 1, :, at : at + CHUNK] = result
            else:
                out_ref[:, at : at + CHUNK] = result


def backward_layers(need_up, h_all, kept, up, g_all, w_vmem, gn, sems):
    q_all, k_all, v_all, p_all = kept
    for layer in reversed(range(LAYERS)):
        acc = jnp.zeros((LENGTH, QW), F32)
        for at in range(0, WIDTH, CHUNK):
            if sems is not None:
                wait_rows(w_vmem, sems, layer, at)
            acc = acc + dot_nn(up[:, at : at + CHUNK], weight_rows(w_vmem, layer, at, KVW, COLS))
        grad_context = stack_heads(acc.astype(BF16))
        query, keys, values, probs = q_all[layer], k_all[layer], v_all[layer], p_all[layer]
        grad_probs = dot_nt(grad_context, values)
        centred = grad_probs - jnp.sum(probs * grad_probs, axis=-1, keepdims=True)
        grad_scores = (probs * centred * SCALE).astype(BF16)
        grad_keys = dot_tn(grad_scores, query).astype(BF16)
        grad_values = dot_tn(probs.astype(BF16), grad_context).astype(BF16)
        if g_all is not None:
            g_all[layer, :, :HEAD] = grad_keys
            g_all[layer, :, HEAD:] = grad_values
        if layer == 0 and not need_up:
            return
        grad_query = unstack_heads(dot_nn(grad_scores, keys).astype(BF16))
        grads = jnp.concatenate([grad_query, grad_keys, grad_values], axis=1)
        inverse = inverse_norm(h_all, layer)
        total = jnp.zeros((LENGTH, 1), F32)
        for at in range(0, WIDTH, CHUNK):
            part = dot_nt(grads, weight_rows(w_vmem, layer, at, 0, KVW))
            gn[:, at : at + CHUNK] = part
            signal = h_all[layer, :, at : at + CHUNK].astype(F32)
            total = total + jnp.sum(part * signal, axis=-1, keepdims=True)
        pull = inverse * inverse * inverse * (total * (1.0 / WIDTH))
        for at in range(0, WIDTH, CHUNK):
            signal = h_all[layer, :, at : at + CHUNK].astype(F32)
            upstream = up[:, at : at + CHUNK].astype(F32)
            up[:, at : at + CHUNK] = (
                upstream + inverse * gn[:, at : at + CHUNK] - signal * pull
            ).astype(BF16)


def first_kernel(place, h_ref, seg_col, seg_row, *refs):
    sources, refs = refs[:SOURCES], refs[SOURCES:]
    out_ref, h_all, n_all, w_vmem, sems = refs
    start_layers(range(LAYERS), place, sources, w_vmem, sems)
    h_all[0] = h_ref[...]
    forward_layers(attention_mask(seg_col, seg_row), h_all, n_all, None, out_ref, w_vmem, sems)


def middle_kernel(place, h_ref, arrived, up_ref, seg_col, seg_row, *refs):
    sources, refs = refs[:SOURCES], refs[SOURCES:]
    out_ref, h_all, n_all, q_all, k_all, v_all, p_all, w_vmem, gn, sems = refs
    start_layers(range(LAYERS), place, sources, w_vmem, sems)

    @pl.when(place[2] == 1)
    def _():
        h_all[0] = arrived[...]

    @pl.when(place[2] == 0)
    def _():
        h_all[0] = h_ref[...]

    out_ref[...] = up_ref[...]
    kept = (q_all, k_all, v_all, p_all)
    forward_layers(attention_mask(seg_col, seg_row), h_all, n_all, kept, None, w_vmem, sems)
    backward_layers(True, h_all, kept, out_ref, None, w_vmem, gn, None)


def last_kernel(place, up_ref, arrived, h_all, q_all, k_all, v_all, p_all, *refs):
    sources, refs = refs[:SOURCES], refs[SOURCES:]
    g_all, up, w_vmem, gn, sems = refs
    start_layers(reversed(range(LAYERS)), place, sources, w_vmem, sems)

    @pl.when(place[2] == 0)
    def _():
        up[...] = arrived[...]

    @pl.when(place[2] == 1)
    def _():
        up[...] = up_ref[...]

    kept = (q_all, k_all, v_all, p_all)
    backward_layers(False, h_all, kept, up, g_all, w_vmem, gn, sems)


VM = pl.BlockSpec(memory_space=pltpu.VMEM)
SM = pl.BlockSpec(memory_space=pltpu.SMEM)
ANY = pl.BlockSpec(memory_space=pl.ANY)
WEIGHT_SCRATCH = pltpu.VMEM((LAYERS, WIDTH // CHUNK, 16, 64, COLS), BF16)
WEIGHT_SEMS = pltpu.SemaphoreType.DMA((LAYERS, WIDTH // CHUNK))
ROWS = jax.ShapeDtypeStruct((LENGTH, WIDTH), BF16)
ROWS_F32 = pltpu.VMEM((LENGTH, WIDTH), F32)
ROWS_ALL = pltpu.VMEM((LAYERS, LENGTH, WIDTH), BF16)
STATE_SHAPES = (
    jax.ShapeDtypeStruct((LAYERS, LENGTH, WIDTH), BF16),
    jax.ShapeDtypeStruct((LAYERS, LENGTH, WIDTH), BF16),
    jax.ShapeDtypeStruct((LAYERS, LENGTH * HEADS, HEAD), BF16),
    jax.ShapeDtypeStruct((LAYERS, LENGTH, HEAD), BF16),
    jax.ShapeDtypeStruct((LAYERS, LENGTH, HEAD), BF16),
    jax.ShapeDtypeStruct((LAYERS, LENGTH * HEADS, LENGTH), F32),
)


def cost(products):
    return pl.CostEstimate(
        flops=products * 2 * LENGTH * WIDTH * COLS,
        bytes_accessed=LAYERS * WIDTH * COLS * 2,
        transcendentals=0,
    )


def call(kernel, name, products, out_shape, inputs, sources, scratch):
    return pl.pallas_call(
        kernel,
        out_shape=out_shape,
        in_specs=[SM] + [VM] * (len(inputs) - 1) + [ANY] * SOURCES,
        out_specs=(VM,) * len(out_shape),
        scratch_shapes=scratch,
        compiler_params=pltpu.CompilerParams(vmem_limit_bytes=VMEM_LIMIT),
        cost_estimate=cost(products),
        name=name,
    )(*inputs, *sources)


def reorder(rows):
    split = rows.reshape(LENGTH, 16, 2, 2, 64)
    return split.transpose(0, 3, 2, 1, 4).reshape(LENGTH, WIDTH)


def swap(block, axis):
    return lax.ppermute(block, axis, [(0, 1), (1, 0)])


def turned(block, distance):
    return lax.ppermute(block, "x", [(i, (i + distance) % 4) for i in range(4)])


def across(block):
    return lax.ppermute(block, ("yh", "yl"), [(i, 3 - i) for i in range(4)])


def gather_layers(pair, rest, c):
    whole = lax.all_gather(pair, ("z", "c"), axis=0).reshape(16, 2, 2, 64, COLS)
    rest = [turned(rest[:, UPPER:], 1), turned(rest[:, UPPER:], 3), turned(rest, 2)]
    rest = jnp.concatenate(rest, axis=1)
    rest = lax.all_gather(rest, ("z", "c"), axis=0).reshape(16, 2, 2, -1, COLS)
    share = lax.dynamic_slice(whole, (0, c, 0, 0, 0), (16, 1, 2, UPPER, COLS))[:, 0]
    early, late = share[:EARLY], share[EARLY:]
    near, far = turned(early, 1), turned(early, 3)
    near, far, late = lax.optimization_barrier((near, far, late))
    near_late, far_late = turned(late, 1), turned(late, 3)
    moved = []
    for block in (near, near_late, far, far_late):
        moved += [block, swap(block, "c")]
    return [whole, rest] + moved


def sum_over(value, axes, count):
    spread = jnp.broadcast_to(value, (count, 8, 128))
    return jnp.sum(lax.all_to_all(spread, axes, 0, 0, tiled=True), axis=0)


def shards(
    inputs, out_grad, doc_ids, query_weight, out_weight, master, first_moment, second_moment
):
    yh, x, yl, c = (lax.axis_index(name) for name in ("yh", "x", "yl", "c"))
    own = jnp.concatenate(
        [
            query_weight[0],
            master[0, 0].astype(BF16),
            master[0, 1].astype(BF16),
            out_weight[0],
        ],
        axis=1,
    )
    segment = lax.dynamic_index_in_dim(doc_ids, x, 0, keepdims=False)
    rows_in = reorder(lax.dynamic_index_in_dim(inputs, x, 0, keepdims=False))
    up_in = reorder(lax.dynamic_index_in_dim(out_grad, x, 0, keepdims=False))
    up_in = swap(up_in, "yl")
    segment = jnp.where(yh == 1, swap(segment, "yl"), segment)
    seg_col, seg_row = segment[:, None], segment[None, :]
    place = jnp.stack([x, c, yh, yl]).astype(jnp.int32)
    with jax.named_scope("gather_weights"):
        pair = jnp.stack([own, swap(own, "yl")])
        tied = lax.optimization_barrier((pair, place, rows_in, up_in, seg_col, seg_row))
        rest, place, rows_in, up_in, seg_col, seg_row = tied
        sources = gather_layers(pair, rest, c)

    (arrived,) = call(
        first_kernel,
        "first_forward",
        LAYERS,
        (ROWS,),
        (place, rows_in, seg_col, seg_row),
        sources,
        [ROWS_ALL, ROWS_ALL, WEIGHT_SCRATCH, WEIGHT_SEMS],
    )
    arrived = across(arrived)
    half_up, h_all, n_all, *kept = call(
        middle_kernel,
        "second_forward_backward",
        2 * LAYERS,
        (ROWS,) + STATE_SHAPES,
        (place, rows_in, arrived, up_in, seg_col, seg_row),
        sources,
        [WEIGHT_SCRATCH, ROWS_F32, WEIGHT_SEMS],
    )
    with jax.named_scope("normed_slices"):
        rows = n_all.reshape(LAYERS, LENGTH, 2, 2, CHUNK).transpose(0, 3, 2, 1, 4)
        rows = rows.reshape(4 * LAYERS, LENGTH, CHUNK)
        rows = lax.all_to_all(rows, PLANE, 0, 0, tiled=True).reshape(-1, CHUNK)
    arrived = across(half_up)
    (grads,) = call(
        last_kernel,
        "first_backward",
        LAYERS,
        (jax.ShapeDtypeStruct((LAYERS, LENGTH, 2 * HEAD), BF16),),
        (place, up_in, arrived, h_all, *kept),
        sources,
        [pltpu.VMEM((LENGTH, WIDTH), BF16), WEIGHT_SCRATCH, ROWS_F32, WEIGHT_SEMS],
    )

    with jax.named_scope("gather_grads"):
        grads, rows = lax.optimization_barrier((grads, rows))
        cols = jnp.broadcast_to(grads[:, None], (LAYERS, 4, LENGTH, 2 * HEAD))
        cols = cols.reshape(4 * LAYERS, LENGTH, 2 * HEAD)
        cols = lax.all_to_all(cols, PLANE, 0, 0, tiled=True).reshape(-1, 2 * HEAD)

    with jax.named_scope("sum_grads"):
        partial = dot_tn(rows, cols).astype(BF16).reshape(16, 64, 2 * HEAD)
        parts = lax.all_to_all(partial, "z", 0, 0, tiled=True)
        grad = jnp.sum(parts.astype(F32), axis=0)
        grad = jnp.stack([grad[:, :HEAD], grad[:, HEAD:]])

    with jax.named_scope("clip"):
        total_sq = sum_over(jnp.sum(grad * grad), "z", 16)
        total_sq = sum_over(total_sq, ("yh",) + PLANE, 32)
        factor = jnp.minimum(1.0, CLIP_NORM / jnp.sqrt(total_sq[0, 0]))
    clipped = grad * factor
    first_new = BETA_FIRST * first_moment[0] + (1.0 - BETA_FIRST) * clipped
    second_new = BETA_SECOND * second_moment[0] + (1.0 - BETA_SECOND) * clipped * clipped
    adam_step = first_new / (jnp.sqrt(second_new) + ADAM_EPSILON)
    fresh_shard = (master[0] - LEARN_RATE * adam_step).astype(BF16)
    return (adam_step[None], fresh_shard[None])


def solution(mesh):
    fine = Mesh(mesh.devices.reshape(tuple(FINE.values())), tuple(FINE))
    section = ("yh", "x")
    placed = (
        P(None, DP, None),
        P(None, DP, None),
        P(None, DP),
        P(section, DP, None),
        P(section, DP, None),
        P(section, None, DP, None),
        P(section, None, DP, None),
        P(section, None, DP, None),
    )
    return jax.shard_map(
        shards,
        mesh=fine,
        in_specs=placed,
        out_specs=(P(section, None, DP, None), P(section, None, DP, None)),
        check_vma=False,
    )
```

```python
import functools
import math

import jax
import jax.numpy as jnp
from jax import lax
from jax.experimental import pallas as pl
from jax.experimental.pallas import tpu as pltpu
from jax.sharding import Mesh, PartitionSpec as P

NORM_EPS = 1e-05
BETA_FIRST = 0.9
BETA_SECOND = 0.95
ADAM_EPSILON = 1e-08
LEARN_RATE = 0.001
CLIP_NORM = 1.0

FINE = {"yh": 2, "x": 4, "z": 16, "yl": 2, "c": 2}
DP = ("z", "yl", "c")
PLANE = ("x", "yl", "c")
LAYERS = 4
LENGTH = 32
WIDTH = 4096
HEAD = 128
HEADS = 4
QW = HEAD * HEADS
KVW = QW + 2 * HEAD
COLS = KVW + QW
CHUNK = 1024
UPPER = 48
EARLY = 8
REST_AT = {1: 0, 3: 64 - UPPER, 2: 2 * (64 - UPPER)}
SOURCES = 10
SCALE = 1.0 / math.sqrt(HEAD)
VMEM_LIMIT = 12 * 1024 * 1024
F32 = jnp.float32
BF16 = jnp.bfloat16


def dot_nn(a, b):
    return lax.dot_general(a, b, (((1,), (0,)), ((), ())), preferred_element_type=F32)


def dot_nt(a, b):
    return lax.dot_general(a, b, (((1,), (1,)), ((), ())), preferred_element_type=F32)


def dot_tn(a, b):
    return lax.dot_general(a, b, (((0,), (0,)), ((), ())), preferred_element_type=F32)


def start_copies(layer, distance, place, sources, weights, sems):
    whole, rest, *moved = sources
    core, side = place[1], place[3]
    for c in range(2):
        for other in range(2):
            at = c * 2 + (side if other == 0 else 1 - side)

            def start(source, first, last, low=0, high=16, at=at):
                target = weights[layer].at[at, low:high, first:last]
                pltpu.make_async_copy(source, target, sems.at[layer, at]).start()

            if distance == 0:
                start(whole.at[:, c, other], 0, 64)
                continue
            begin = REST_AT[distance]
            first = 0 if distance == 2 else UPPER
            start(rest.at[:, c, other, begin : begin + 64 - first], first, 64)
            if distance == 2:
                continue
            for own in range(2):

                @pl.when((core == c) == (own == 0))
                def _(own=own, other=other, start=start):
                    early, late = moved[(distance // 2) * 4 + own], moved[(distance // 2) * 4 + 2 + own]
                    start(early.at[:, other], 0, UPPER, 0, EARLY)
                    start(late.at[:, other], 0, UPPER, EARLY, 16)


def start_layers(order, place, sources, weights, sems):
    x = place[0]
    for layer in order:
        for distance in range(4):

            @pl.when(((x - layer + 4) & 3) == distance)
            def _(layer=layer, distance=distance):
                start_copies(layer, distance, place, sources, weights, sems)


def wait_rows(weights, sems, layer, at):
    block = weights[layer].at[at // CHUNK]
    pltpu.make_async_copy(block, block, sems.at[layer, at // CHUNK]).wait()


def stack_heads(rows):
    return jnp.concatenate([rows[:, h * HEAD : (h + 1) * HEAD] for h in range(HEADS)], axis=0)


def unstack_heads(rows):
    return jnp.concatenate([rows[h * LENGTH : (h + 1) * LENGTH] for h in range(HEADS)], axis=1)


def weight_rows(weights, layer, at, first, last):
    block = weights[layer][at // CHUNK, :, :, first:last]
    return block.reshape(CHUNK, last - first)


def attention_mask(seg_col, seg_row):
    row_ids = lax.broadcasted_iota(jnp.int32, (LENGTH, LENGTH), 0)
    col_ids = lax.broadcasted_iota(jnp.int32, (LENGTH, LENGTH), 1)
    allowed = ((seg_col[...] == seg_row[...]) & (col_ids <= row_ids)).astype(F32)
    return jnp.concatenate([allowed] * HEADS, axis=0) > 0.0


def forward_layers(mask, h_all, kept, out_ref, weights, sems):
    def project(layer, at, rows, acc, squares):
        if sems is not None:
            wait_rows(weights, sems, layer, at)
        wide = rows.astype(F32)
        acc = acc + dot_nn(rows, weight_rows(weights, layer, at, 0, KVW))
        return acc, squares + jnp.sum(wide * wide, axis=-1, keepdims=True)

    start = (jnp.zeros((LENGTH, KVW), F32), jnp.zeros((LENGTH, 1), F32))
    acc, squares = start
    for at in range(0, WIDTH, CHUNK):
        acc, squares = project(0, at, h_all[0, :, at : at + CHUNK], acc, squares)
    for layer in range(LAYERS):
        inverse = lax.rsqrt(squares * (1.0 / WIDTH) + NORM_EPS)
        rows = (acc * inverse).astype(BF16)
        query = stack_heads(rows[:, :QW])
        keys = rows[:, QW : QW + HEAD]
        values = rows[:, QW + HEAD :]
        scores = dot_nt(query, keys) * SCALE
        exp_scores = jnp.where(mask, jnp.exp(scores), 0.0)
        probs = exp_scores / jnp.sum(exp_scores, axis=-1, keepdims=True)
        if kept is not None:
            n_all, i_all, q_all, k_all, v_all, p_all = kept
            for ref, value in zip(kept[2:], (query, keys, values, probs)):
                ref[layer] = value
            i_all[layer] = jnp.broadcast_to(inverse, (LENGTH, HEAD))
            for at in range(0, WIDTH, CHUNK):
                signal = h_all[layer, :, at : at + CHUNK].astype(F32)
                core, side = divmod(at // CHUNK, 2)
                n_all[layer * 4 + side * 2 + core] = (signal * inverse).astype(BF16)
        if out_ref is None and layer + 1 == LAYERS:
            return
        context = unstack_heads(dot_nn(probs.astype(BF16), values).astype(BF16))
        acc, squares = start
        for at in range(0, WIDTH, CHUNK):
            signal = h_all[layer, :, at : at + CHUNK].astype(F32)
            branch = dot_nt(context, weight_rows(weights, layer, at, KVW, COLS))
            result = (signal + branch).astype(BF16)
            if layer + 1 < LAYERS:
                h_all[layer + 1, :, at : at + CHUNK] = result
                acc, squares = project(layer + 1, at, result, acc, squares)
            else:
                out_ref[:, at : at + CHUNK] = result


def backward_layers(need_up, h_all, kept, up, g_all, weights):
    i_all, q_all, k_all, v_all, p_all = kept

    def project(layer, at, rows, acc):
        return acc + dot_nn(rows, weight_rows(weights, layer, at, KVW, COLS))

    acc = jnp.zeros((LENGTH, QW), F32)
    for at in range(0, WIDTH, CHUNK):
        acc = project(LAYERS - 1, at, up[:, at : at + CHUNK], acc)
    for layer in reversed(range(LAYERS)):
        grad_context = stack_heads(acc.astype(BF16))
        query, keys, values, probs = q_all[layer], k_all[layer], v_all[layer], p_all[layer]
        grad_probs = dot_nt(grad_context, values)
        centred = grad_probs - jnp.sum(probs * grad_probs, axis=-1, keepdims=True)
        grad_scores = (probs * centred * SCALE).astype(BF16)
        grad_keys = dot_tn(grad_scores, query).astype(BF16)
        grad_values = dot_tn(probs.astype(BF16), grad_context).astype(BF16)
        if g_all is not None:
            for copy in range(4):
                g_all[layer * 4 + copy, :, :HEAD] = grad_keys
                g_all[layer * 4 + copy, :, HEAD:] = grad_values
        if layer == 0 and not need_up:
            return
        grad_query = dot_nn(grad_scores, keys).astype(BF16)
        grads = jnp.concatenate([unstack_heads(grad_query), grad_keys, grad_values], axis=1)
        by_head = jnp.sum(grad_query.astype(F32) * query.astype(F32), axis=-1, keepdims=True)
        total = sum(by_head[h * LENGTH : (h + 1) * LENGTH] for h in range(HEADS))
        for grad, value in ((grad_keys, keys), (grad_values, values)):
            product = grad.astype(F32) * value.astype(F32)
            total = total + jnp.sum(product, axis=-1, keepdims=True)
        inverse = i_all[layer][:, :1]
        pull = inverse * inverse * (total * (1.0 / WIDTH))
        acc = jnp.zeros((LENGTH, QW), F32)
        for at in range(0, WIDTH, CHUNK):
            part = dot_nt(grads, weight_rows(weights, layer, at, 0, KVW))
            signal = h_all[layer, :, at : at + CHUNK].astype(F32)
            upstream = up[:, at : at + CHUNK].astype(F32)
            result = (upstream + inverse * part - signal * pull).astype(BF16)
            up[:, at : at + CHUNK] = result
            if layer > 0:
                acc = project(layer - 1, at, result, acc)


def first_kernel(place, h_ref, seg_col, seg_row, *refs):
    sources, refs = refs[:SOURCES], refs[SOURCES:]
    out_ref, *weights = refs[: LAYERS + 1]
    h_all, sems = refs[LAYERS + 1 :]
    start_layers(range(LAYERS), place, sources, weights, sems)
    h_all[0] = h_ref[...]
    mask = attention_mask(seg_col, seg_row)
    forward_layers(mask, h_all, None, out_ref, weights, sems)


def middle_kernel(place, h_ref, arrived, up_ref, seg_col, seg_row, *refs):
    weights, refs = refs[:LAYERS], refs[LAYERS:]
    out_ref, h_all, *kept = refs

    @pl.when(place[2] == 1)
    def _():
        h_all[0] = arrived[...]

    @pl.when(place[2] == 0)
    def _():
        h_all[0] = h_ref[...]

    out_ref[...] = up_ref[...]
    mask = attention_mask(seg_col, seg_row)
    forward_layers(mask, h_all, kept, None, weights, None)
    backward_layers(True, h_all, kept[1:], out_ref, None, weights)


def last_kernel(place, up_ref, arrived, h_all, i_all, q_all, k_all, v_all, p_all, *refs):
    weights, refs = refs[:LAYERS], refs[LAYERS:]
    g_all, up = refs

    @pl.when(place[2] == 0)
    def _():
        up[...] = arrived[...]

    @pl.when(place[2] == 1)
    def _():
        up[...] = up_ref[...]

    kept = (i_all, q_all, k_all, v_all, p_all)
    backward_layers(False, h_all, kept, up, g_all, weights)


VM = pl.BlockSpec(memory_space=pltpu.VMEM)
SM = pl.BlockSpec(memory_space=pltpu.SMEM)
ANY = pl.BlockSpec(memory_space=pl.ANY)
WEIGHTS = (pltpu.VMEM((WIDTH // CHUNK, 16, 64, COLS), BF16),) * LAYERS
WEIGHT_SEMS = pltpu.SemaphoreType.DMA((LAYERS, WIDTH // CHUNK))
ROWS = jax.ShapeDtypeStruct((LENGTH, WIDTH), BF16)
ROWS_ALL = pltpu.VMEM((LAYERS, LENGTH, WIDTH), BF16)
STATE_SHAPES = (
    jax.ShapeDtypeStruct((LAYERS, LENGTH, WIDTH), BF16),
    jax.ShapeDtypeStruct((LAYERS * 4, LENGTH, CHUNK), BF16),
    jax.ShapeDtypeStruct((LAYERS, LENGTH, HEAD), F32),
    jax.ShapeDtypeStruct((LAYERS, LENGTH * HEADS, HEAD), BF16),
    jax.ShapeDtypeStruct((LAYERS, LENGTH, HEAD), BF16),
    jax.ShapeDtypeStruct((LAYERS, LENGTH, HEAD), BF16),
    jax.ShapeDtypeStruct((LAYERS, LENGTH * HEADS, LENGTH), F32),
)


def cost(products):
    return pl.CostEstimate(
        flops=products * 2 * LENGTH * WIDTH * COLS,
        bytes_accessed=LAYERS * WIDTH * COLS * 2,
        transcendentals=0,
    )


def call(kernel, name, products, out_shape, inputs, sources, scratch):
    return pl.pallas_call(
        kernel,
        out_shape=out_shape,
        in_specs=[SM] + [VM] * (len(inputs) - 1) + [ANY] * len(sources),
        out_specs=(VM,) * len(out_shape),
        scratch_shapes=scratch,
        compiler_params=pltpu.CompilerParams(vmem_limit_bytes=VMEM_LIMIT),
        cost_estimate=cost(products),
        name=name,
    )(*inputs, *sources)


def reorder(rows):
    split = rows.reshape(LENGTH, 16, 2, 2, 64)
    return split.transpose(0, 3, 2, 1, 4).reshape(LENGTH, WIDTH)


def swap(block, axis):
    return lax.ppermute(block, axis, [(0, 1), (1, 0)])


def turned(block, distance):
    return lax.ppermute(block, "x", [(i, (i + distance) % 4) for i in range(4)])


def across(block):
    return lax.ppermute(block, ("yh", "yl"), [(i, 3 - i) for i in range(4)])


def gather_layers(pair, rest, c):
    whole = lax.all_gather(pair, ("z", "c"), axis=0).reshape(16, 2, 2, 64, COLS)
    rest = [turned(rest[:, UPPER:], 1), turned(rest[:, UPPER:], 3), turned(rest, 2)]
    rest = jnp.concatenate(rest, axis=1)
    rest = lax.all_gather(rest, ("z", "c"), axis=0).reshape(16, 2, 2, -1, COLS)
    share = lax.dynamic_slice(whole, (0, c, 0, 0, 0), (16, 1, 2, UPPER, COLS))[:, 0]
    early, late = share[:EARLY], share[EARLY:]
    near, far = turned(early, 1), turned(early, 3)
    near, far, late = lax.optimization_barrier((near, far, late))
    near_late, far_late = turned(late, 1), turned(late, 3)
    moved = []
    for block in (near, near_late, far, far_late):
        moved += [block, swap(block, "c")]
    return [whole, rest] + moved


def sum_over(value, axes, count):
    spread = jnp.broadcast_to(value, (count, 8, 128))
    return jnp.sum(lax.all_to_all(spread, axes, 0, 0, tiled=True), axis=0)


def shards(
    inputs, out_grad, doc_ids, query_weight, out_weight, master, first_moment, second_moment
):
    yh, x, yl, c = (lax.axis_index(name) for name in ("yh", "x", "yl", "c"))
    own = jnp.concatenate(
        [
            query_weight[0],
            master[0, 0].astype(BF16),
            master[0, 1].astype(BF16),
            out_weight[0],
        ],
        axis=1,
    )
    segment = lax.dynamic_index_in_dim(doc_ids, x, 0, keepdims=False)
    rows_in = reorder(lax.dynamic_index_in_dim(inputs, x, 0, keepdims=False))
    up_in = reorder(lax.dynamic_index_in_dim(out_grad, x, 0, keepdims=False))
    up_in = swap(up_in, "yl")
    segment = jnp.where(yh == 1, swap(segment, "yl"), segment)
    seg_col, seg_row = segment[:, None], segment[None, :]
    place = jnp.stack([x, c, yh, yl]).astype(jnp.int32)
    with jax.named_scope("gather_weights"):
        pair = jnp.stack([own, swap(own, "yl")])
        tied = lax.optimization_barrier((pair, place, rows_in, up_in, seg_col, seg_row))
        rest, place, rows_in, up_in, seg_col, seg_row = tied
        sources = gather_layers(pair, rest, c)

    arrived, *weights = call(
        first_kernel,
        "first_forward",
        LAYERS,
        (ROWS,) + WEIGHTS,
        (place, rows_in, seg_col, seg_row),
        sources,
        [ROWS_ALL, WEIGHT_SEMS],
    )
    weights = [pltpu.with_memory_space_constraint(block, pltpu.VMEM) for block in weights]
    arrived = across(arrived)
    half_up, h_all, n_all, *kept = call(
        middle_kernel,
        "second_forward_backward",
        2 * LAYERS,
        (ROWS,) + STATE_SHAPES,
        (place, rows_in, arrived, up_in, seg_col, seg_row, *weights),
        (),
        [],
    )
    with jax.named_scope("normed_slices"):
        rows = lax.all_to_all(n_all, PLANE, 0, 0, tiled=True).reshape(-1, CHUNK)
    arrived = across(half_up)
    (grads,) = call(
        last_kernel,
        "first_backward",
        LAYERS,
        (jax.ShapeDtypeStruct((LAYERS * 4, LENGTH, 2 * HEAD), BF16),),
        (place, up_in, arrived, h_all, *kept, *weights),
        (),
        [pltpu.VMEM((LENGTH, WIDTH), BF16)],
    )

    with jax.named_scope("gather_grads"):
        grads, rows = lax.optimization_barrier((grads, rows))
        cols = lax.all_to_all(grads, PLANE, 0, 0, tiled=True).reshape(-1, 2 * HEAD)

    with jax.named_scope("sum_grads"):
        partial = dot_tn(rows, cols).astype(BF16).reshape(16, 64, 2 * HEAD)
        parts = lax.all_to_all(partial, "z", 0, 0, tiled=True)
        grad = jnp.sum(parts.astype(F32), axis=0)
        grad = jnp.stack([grad[:, :HEAD], grad[:, HEAD:]])

    with jax.named_scope("clip"):
        total_sq = sum_over(jnp.sum(grad * grad), "z", 16)
        total_sq = sum_over(total_sq, ("yh",) + PLANE, 32)
        factor = jnp.minimum(1.0, CLIP_NORM / jnp.sqrt(total_sq[0, 0]))
    clipped = grad * factor
    first_new = BETA_FIRST * first_moment[0] + (1.0 - BETA_FIRST) * clipped
    second_new = BETA_SECOND * second_moment[0] + (1.0 - BETA_SECOND) * clipped * clipped
    adam_step = first_new / (jnp.sqrt(second_new) + ADAM_EPSILON)
    fresh_shard = (master[0] - LEARN_RATE * adam_step).astype(BF16)
    return (adam_step[None], fresh_shard[None])


def solution(mesh):
    fine = Mesh(mesh.devices.reshape(tuple(FINE.values())), tuple(FINE))
    section = ("yh", "x")
    placed = (
        P(None, DP, None),
        P(None, DP, None),
        P(None, DP),
        P(section, DP, None),
        P(section, DP, None),
        P(section, None, DP, None),
        P(section, None, DP, None),
        P(section, None, DP, None),
    )
    return jax.shard_map(
        shards,
        mesh=fine,
        in_specs=placed,
        out_specs=(P(section, None, DP, None), P(section, None, DP, None)),
        check_vma=False,
    )
```

```python
import functools
import math

import jax
import jax.numpy as jnp
from jax import lax
from jax.experimental import pallas as pl
from jax.experimental.pallas import tpu as pltpu
from jax.sharding import Mesh, PartitionSpec as P

NORM_EPS = 1e-05
BETA_FIRST = 0.9
BETA_SECOND = 0.95
ADAM_EPSILON = 1e-08
LEARN_RATE = 0.001
CLIP_NORM = 1.0

FINE = {"yh": 2, "x": 4, "z": 16, "yl": 2, "c": 2}
DP = ("z", "yl", "c")
PLANE = ("x", "yl", "c")
LAYERS = 4
LENGTH = 32
WIDTH = 4096
HEAD = 128
HEADS = 4
QW = HEAD * HEADS
KVW = QW + 2 * HEAD
COLS = KVW + QW
CHUNK = 1024
ALONG_X = 896
EARLY = 10
REST_AT = {1: 0, 3: COLS - ALONG_X, 2: 2 * (COLS - ALONG_X)}
SOURCES = 10
SCALE = 1.0 / math.sqrt(HEAD)
VMEM_LIMIT = 12 * 1024 * 1024
VMEM_LAST = 56 * 1024 * 1024
F32 = jnp.float32
BF16 = jnp.bfloat16


def dot_nn(a, b):
    return lax.dot_general(a, b, (((1,), (0,)), ((), ())), preferred_element_type=F32)


def dot_nt(a, b):
    return lax.dot_general(a, b, (((1,), (1,)), ((), ())), preferred_element_type=F32)


def dot_tn(a, b):
    return lax.dot_general(a, b, (((0,), (0,)), ((), ())), preferred_element_type=F32)


def start_copies(layer, distance, place, sources, weights, sems):
    whole, rest, *moved = sources
    core, side = place[1], place[3]
    for c in range(2):
        for other in range(2):
            at = c * 2 + (side if other == 0 else 1 - side)

            def start(source, first, last, low=0, high=16, at=at):
                target = weights[layer].at[at, low:high, :, first:last]
                pltpu.make_async_copy(source, target, sems.at[layer, at]).start()

            if distance == 0:
                start(whole.at[:, c, other], 0, COLS)
                continue
            begin = REST_AT[distance]
            first = 0 if distance == 2 else ALONG_X
            start(rest.at[:, c, other, :, begin : begin + COLS - first], first, COLS)
            if distance == 2:
                continue
            for own in range(2):

                @pl.when((core == c) == (own == 0))
                def _(own=own, other=other, start=start):
                    early, late = moved[(distance // 2) * 4 + own], moved[(distance // 2) * 4 + 2 + own]
                    start(early.at[:, other], 0, ALONG_X, 0, EARLY)
                    start(late.at[:, other], 0, ALONG_X, EARLY, 16)


def start_layers(order, place, sources, weights, sems):
    x = place[0]
    for layer in order:
        for distance in range(4):

            @pl.when(((x - layer + 4) & 3) == distance)
            def _(layer=layer, distance=distance):
                start_copies(layer, distance, place, sources, weights, sems)


def wait_rows(weights, sems, layer, at):
    block = weights[layer].at[at // CHUNK]
    pltpu.make_async_copy(block, block, sems.at[layer, at // CHUNK]).wait()


def stack_heads(rows):
    return jnp.concatenate([rows[:, h * HEAD : (h + 1) * HEAD] for h in range(HEADS)], axis=0)


def unstack_heads(rows):
    return jnp.concatenate([rows[h * LENGTH : (h + 1) * LENGTH] for h in range(HEADS)], axis=1)


def weight_rows(weights, layer, at, first, last):
    block = weights[layer][at // CHUNK, :, :, first:last]
    return block.reshape(CHUNK, last - first)


def attention_mask(seg_col, seg_row):
    row_ids = lax.broadcasted_iota(jnp.int32, (LENGTH, LENGTH), 0)
    col_ids = lax.broadcasted_iota(jnp.int32, (LENGTH, LENGTH), 1)
    allowed = ((seg_col[...] == seg_row[...]) & (col_ids <= row_ids)).astype(F32)
    return jnp.concatenate([allowed] * HEADS, axis=0) > 0.0


def forward_layers(mask, h_all, kept, out_ref, weights, sems):
    def project(layer, at, rows, acc, squares):
        if sems is not None:
            wait_rows(weights, sems, layer, at)
        wide = rows.astype(F32)
        acc = acc + dot_nn(rows, weight_rows(weights, layer, at, 0, KVW))
        return acc, squares + jnp.sum(wide * wide, axis=-1, keepdims=True)

    start = (jnp.zeros((LENGTH, KVW), F32), jnp.zeros((LENGTH, 1), F32))
    acc, squares = start
    for at in range(0, WIDTH, CHUNK):
        acc, squares = project(0, at, h_all[0, :, at : at + CHUNK], acc, squares)
    for layer in range(LAYERS):
        inverse = lax.rsqrt(squares * (1.0 / WIDTH) + NORM_EPS)
        rows = (acc * inverse).astype(BF16)
        query = stack_heads(rows[:, :QW])
        keys = rows[:, QW : QW + HEAD]
        values = rows[:, QW + HEAD :]
        scores = dot_nt(query, keys) * SCALE
        exp_scores = jnp.where(mask, jnp.exp(scores), 0.0)
        probs = exp_scores / jnp.sum(exp_scores, axis=-1, keepdims=True)
        if kept is not None:
            n_all, i_all, q_all, k_all, v_all, p_all = kept
            for ref, value in zip(kept[2:], (query, keys, values, probs)):
                ref[layer] = value
            i_all[layer] = jnp.broadcast_to(inverse, (LENGTH, HEAD))
            for at in range(0, WIDTH, CHUNK):
                signal = h_all[layer, :, at : at + CHUNK].astype(F32)
                core, side = divmod(at // CHUNK, 2)
                n_all[layer * 4 + side * 2 + core] = (signal * inverse).astype(BF16)
        if out_ref is None and layer + 1 == LAYERS:
            return
        context = unstack_heads(dot_nn(probs.astype(BF16), values).astype(BF16))
        acc, squares = start
        for at in range(0, WIDTH, CHUNK):
            signal = h_all[layer, :, at : at + CHUNK].astype(F32)
            branch = dot_nt(context, weight_rows(weights, layer, at, KVW, COLS))
            result = (signal + branch).astype(BF16)
            if layer + 1 < LAYERS:
                h_all[layer + 1, :, at : at + CHUNK] = result
                acc, squares = project(layer + 1, at, result, acc, squares)
            else:
                out_ref[:, at : at + CHUNK] = result


def backward_layers(need_up, h_all, kept, up, g_all, weights, sems):
    i_all, q_all, k_all, v_all, p_all = kept

    def project(layer, at, rows, acc):
        if sems is not None:
            wait_rows(weights, sems, layer, at)
        return acc + dot_nn(rows, weight_rows(weights, layer, at, KVW, COLS))

    acc = jnp.zeros((LENGTH, QW), F32)
    for at in range(0, WIDTH, CHUNK):
        acc = project(LAYERS - 1, at, up[:, at : at + CHUNK], acc)
    for layer in reversed(range(LAYERS)):
        grad_context = stack_heads(acc.astype(BF16))
        query, keys, values, probs = q_all[layer], k_all[layer], v_all[layer], p_all[layer]
        grad_probs = dot_nt(grad_context, values)
        centred = grad_probs - jnp.sum(probs * grad_probs, axis=-1, keepdims=True)
        grad_scores = (probs * centred * SCALE).astype(BF16)
        grad_keys = dot_tn(grad_scores, query).astype(BF16)
        grad_values = dot_tn(probs.astype(BF16), grad_context).astype(BF16)
        if g_all is not None:
            for copy in range(4):
                g_all[layer * 4 + copy, :, :HEAD] = grad_keys
                g_all[layer * 4 + copy, :, HEAD:] = grad_values
        if layer == 0 and not need_up:
            return
        grad_query = dot_nn(grad_scores, keys).astype(BF16)
        grads = jnp.concatenate([unstack_heads(grad_query), grad_keys, grad_values], axis=1)
        by_head = jnp.sum(grad_query.astype(F32) * query.astype(F32), axis=-1, keepdims=True)
        total = sum(by_head[h * LENGTH : (h + 1) * LENGTH] for h in range(HEADS))
        for grad, value in ((grad_keys, keys), (grad_values, values)):
            product = grad.astype(F32) * value.astype(F32)
            total = total + jnp.sum(product, axis=-1, keepdims=True)
        inverse = i_all[layer][:, :1]
        pull = inverse * inverse * (total * (1.0 / WIDTH))
        acc = jnp.zeros((LENGTH, QW), F32)
        for at in range(0, WIDTH, CHUNK):
            part = dot_nt(grads, weight_rows(weights, layer, at, 0, KVW))
            signal = h_all[layer, :, at : at + CHUNK].astype(F32)
            upstream = up[:, at : at + CHUNK].astype(F32)
            result = (upstream + inverse * part - signal * pull).astype(BF16)
            up[:, at : at + CHUNK] = result
            if layer > 0:
                acc = project(layer - 1, at, result, acc)


def first_kernel(place, h_ref, seg_col, seg_row, *refs):
    sources, refs = refs[:SOURCES], refs[SOURCES:]
    out_ref, *weights = refs[: LAYERS + 1]
    h_all, sems = refs[LAYERS + 1 :]
    start_layers(range(LAYERS), place, sources, weights, sems)
    h_all[0] = h_ref[...]
    mask = attention_mask(seg_col, seg_row)
    forward_layers(mask, h_all, None, out_ref, weights, sems)


def middle_kernel(place, h_ref, arrived, up_ref, seg_col, seg_row, *refs):
    weights, refs = refs[:LAYERS], refs[LAYERS:]
    out_ref, h_all, *kept = refs

    @pl.when(place[2] == 1)
    def _():
        h_all[0] = arrived[...]

    @pl.when(place[2] == 0)
    def _():
        h_all[0] = h_ref[...]

    out_ref[...] = up_ref[...]
    mask = attention_mask(seg_col, seg_row)
    forward_layers(mask, h_all, kept, None, weights, None)
    backward_layers(True, h_all, kept[1:], out_ref, None, weights, None)


def last_kernel(place, up_ref, arrived, h_all, i_all, q_all, k_all, v_all, p_all, *refs):
    sources, refs = refs[:SOURCES], refs[SOURCES:]
    g_all, up, sems, *weights = refs
    start_layers(reversed(range(LAYERS)), place, sources, weights, sems)

    @pl.when(place[2] == 0)
    def _():
        up[...] = arrived[...]

    @pl.when(place[2] == 1)
    def _():
        up[...] = up_ref[...]

    kept = (i_all, q_all, k_all, v_all, p_all)
    backward_layers(False, h_all, kept, up, g_all, weights, sems)


VM = pl.BlockSpec(memory_space=pltpu.VMEM)
SM = pl.BlockSpec(memory_space=pltpu.SMEM)
ANY = pl.BlockSpec(memory_space=pl.ANY)
WEIGHTS = (pltpu.VMEM((WIDTH // CHUNK, 16, 64, COLS), BF16),) * LAYERS
WEIGHT_SEMS = pltpu.SemaphoreType.DMA((LAYERS, WIDTH // CHUNK))
ROWS = jax.ShapeDtypeStruct((LENGTH, WIDTH), BF16)
ROWS_ALL = pltpu.VMEM((LAYERS, LENGTH, WIDTH), BF16)
STATE_SHAPES = (
    pltpu.HBM((LAYERS, LENGTH, WIDTH), BF16),
    pltpu.HBM((LAYERS * 4, LENGTH, CHUNK), BF16),
    pltpu.HBM((LAYERS, LENGTH, HEAD), F32),
    pltpu.HBM((LAYERS, LENGTH * HEADS, HEAD), BF16),
    pltpu.HBM((LAYERS, LENGTH, HEAD), BF16),
    pltpu.HBM((LAYERS, LENGTH, HEAD), BF16),
    pltpu.HBM((LAYERS, LENGTH * HEADS, LENGTH), F32),
)


def cost(products):
    return pl.CostEstimate(
        flops=products * 2 * LENGTH * WIDTH * COLS,
        bytes_accessed=LAYERS * WIDTH * COLS * 2,
        transcendentals=0,
    )


def call(
    kernel, name, products, out_shape, inputs, sources, scratch, limit=VMEM_LIMIT
):
    return pl.pallas_call(
        kernel,
        out_shape=out_shape,
        in_specs=[SM] + [VM] * (len(inputs) - 1) + [ANY] * len(sources),
        out_specs=(VM,) * len(out_shape),
        scratch_shapes=scratch,
        compiler_params=pltpu.CompilerParams(vmem_limit_bytes=limit),
        cost_estimate=cost(products),
        name=name,
    )(*inputs, *sources)


def reorder(rows):
    split = rows.reshape(LENGTH, 16, 2, 2, 64)
    return split.transpose(0, 3, 2, 1, 4).reshape(LENGTH, WIDTH)


def swap(block, axis):
    return lax.ppermute(block, axis, [(0, 1), (1, 0)])


def turned(block, distance):
    return lax.ppermute(block, "x", [(i, (i + distance) % 4) for i in range(4)])


def across(block):
    return lax.ppermute(block, ("yh", "yl"), [(i, 3 - i) for i in range(4)])


def gather_layers(pair, rest, c):
    whole = lax.all_gather(pair, ("z", "c"), axis=0).reshape(16, 2, 2, 64, COLS)
    edge = rest[:, :, ALONG_X:]
    rest = jnp.concatenate([turned(edge, 1), turned(edge, 3), turned(rest, 2)], axis=2)
    rest = lax.all_gather(rest, ("z", "c"), axis=0).reshape(16, 2, 2, 64, -1)
    share = lax.dynamic_slice(whole, (0, c, 0, 0, 0), (16, 1, 2, 64, ALONG_X))[:, 0]
    early, late = share[:EARLY], share[EARLY:]
    near, far = turned(early, 1), turned(early, 3)
    near, late_near = lax.optimization_barrier((near, late))
    far, late_far = lax.optimization_barrier((far, late))
    near_late, far_late = turned(late_near, 1), turned(late_far, 3)
    moved = []
    for block in (near, near_late, far, far_late):
        moved += [block, swap(block, "c")]
    return [whole, rest] + moved


def sum_over(value, axes, count):
    spread = jnp.broadcast_to(value, (count, 8, 128))
    return jnp.sum(lax.all_to_all(spread, axes, 0, 0, tiled=True), axis=0)


def shards(
    inputs, out_grad, doc_ids, query_weight, out_weight, master, first_moment, second_moment
):
    yh, x, yl, c = (lax.axis_index(name) for name in ("yh", "x", "yl", "c"))
    own = jnp.concatenate(
        [
            query_weight[0],
            master[0, 0].astype(BF16),
            master[0, 1].astype(BF16),
            out_weight[0],
        ],
        axis=1,
    )
    segment = lax.dynamic_index_in_dim(doc_ids, x, 0, keepdims=False)
    rows_in = reorder(lax.dynamic_index_in_dim(inputs, x, 0, keepdims=False))
    up_in = reorder(lax.dynamic_index_in_dim(out_grad, x, 0, keepdims=False))
    up_in = swap(up_in, "yl")
    segment = jnp.where(yh == 1, swap(segment, "yl"), segment)
    seg_col, seg_row = segment[:, None], segment[None, :]
    place = jnp.stack([x, c, yh, yl]).astype(jnp.int32)
    with jax.named_scope("gather_weights"):
        pair = jnp.stack([own, swap(own, "yl")])
        tied = lax.optimization_barrier((pair, place, rows_in, up_in, seg_col, seg_row))
        rest, place, rows_in, up_in, seg_col, seg_row = tied
        sources = gather_layers(pair, rest, c)

    arrived, *weights = call(
        first_kernel,
        "first_forward",
        LAYERS,
        (ROWS,) + WEIGHTS,
        (place, rows_in, seg_col, seg_row),
        sources,
        [ROWS_ALL, WEIGHT_SEMS],
    )
    weights = [pltpu.with_memory_space_constraint(block, pltpu.VMEM) for block in weights]
    arrived = across(arrived)
    half_up, h_all, n_all, *kept = call(
        middle_kernel,
        "second_forward_backward",
        2 * LAYERS,
        (ROWS,) + STATE_SHAPES,
        (place, rows_in, arrived, up_in, seg_col, seg_row, *weights),
        (),
        [],
    )
    with jax.named_scope("normed_slices"):
        rows = lax.all_to_all(n_all, PLANE, 0, 0, tiled=True).reshape(-1, CHUNK)
    arrived = across(half_up)
    (grads,) = call(
        last_kernel,
        "first_backward",
        LAYERS,
        (jax.ShapeDtypeStruct((LAYERS * 4, LENGTH, 2 * HEAD), BF16),),
        (place, up_in, arrived, h_all, *kept),
        sources,
        [pltpu.VMEM((LENGTH, WIDTH), BF16), WEIGHT_SEMS, *WEIGHTS],
        VMEM_LAST,
    )

    with jax.named_scope("gather_grads"):
        grads, rows = lax.optimization_barrier((grads, rows))
        cols = lax.all_to_all(grads, PLANE, 0, 0, tiled=True).reshape(-1, 2 * HEAD)

    with jax.named_scope("sum_grads"):
        partial = dot_tn(rows, cols).astype(BF16).reshape(16, 64, 2 * HEAD)
        parts = lax.all_to_all(partial, "z", 0, 0, tiled=True)
        grad = jnp.sum(parts.astype(F32), axis=0)
        grad = jnp.stack([grad[:, :HEAD], grad[:, HEAD:]])

    with jax.named_scope("clip"):
        total_sq = sum_over(jnp.sum(grad * grad), "z", 16)
        total_sq = sum_over(total_sq, ("yh",) + PLANE, 32)
        factor = jnp.minimum(1.0, CLIP_NORM / jnp.sqrt(total_sq[0, 0]))
    clipped = grad * factor
    first_new = BETA_FIRST * first_moment[0] + (1.0 - BETA_FIRST) * clipped
    second_new = BETA_SECOND * second_moment[0] + (1.0 - BETA_SECOND) * clipped * clipped
    adam_step = first_new / (jnp.sqrt(second_new) + ADAM_EPSILON)
    fresh_shard = (master[0] - LEARN_RATE * adam_step).astype(BF16)
    return (adam_step[None], fresh_shard[None])


def solution(mesh):
    fine = Mesh(mesh.devices.reshape(tuple(FINE.values())), tuple(FINE))
    section = ("yh", "x")
    placed = (
        P(None, DP, None),
        P(None, DP, None),
        P(None, DP),
        P(section, DP, None),
        P(section, DP, None),
        P(section, None, DP, None),
        P(section, None, DP, None),
        P(section, None, DP, None),
    )
    return jax.shard_map(
        shards,
        mesh=fine,
        in_specs=placed,
        out_specs=(P(section, None, DP, None), P(section, None, DP, None)),
        check_vma=False,
    )
```

```python
import functools
import math

import jax
import jax.numpy as jnp
from jax import lax
from jax.experimental import pallas as pl
from jax.experimental.pallas import tpu as pltpu
from jax.sharding import Mesh, PartitionSpec as P

NORM_EPS = 1e-05
BETA_FIRST = 0.9
BETA_SECOND = 0.95
ADAM_EPSILON = 1e-08
LEARN_RATE = 0.001
CLIP_NORM = 1.0

FINE = {"yh": 2, "x": 4, "z": 16, "yl": 2, "c": 2}
DP = ("z", "yl", "c")
PLANE = ("x", "yl", "c")
LAYERS = 4
LENGTH = 32
WIDTH = 4096
HEAD = 128
HEADS = 4
QW = HEAD * HEADS
KVW = QW + 2 * HEAD
COLS = KVW + QW
CHUNK = 1024
LOADED = 1
ALONG_X = 896
EARLY = 10
REST_AT = {1: 0, 3: COLS - ALONG_X, 2: 2 * (COLS - ALONG_X)}
SOURCES = 10
SCALE = 1.0 / math.sqrt(HEAD)
VMEM_LIMIT = 7 * 1024 * 1024
VMEM_LAST = 37 * 1024 * 1024
F32 = jnp.float32
BF16 = jnp.bfloat16


def dot_nn(a, b):
    return lax.dot_general(a, b, (((1,), (0,)), ((), ())), preferred_element_type=F32)


def dot_nt(a, b):
    return lax.dot_general(a, b, (((1,), (1,)), ((), ())), preferred_element_type=F32)


def dot_tn(a, b):
    return lax.dot_general(a, b, (((0,), (0,)), ((), ())), preferred_element_type=F32)


def start_copies(layer, distance, place, sources, weights, sems):
    whole, rest, *moved = sources
    core, side = place[1], place[3]
    for c in range(2):
        for other in range(2):
            at = c * 2 + (side if other == 0 else 1 - side)

            def start(source, first, last, low=0, high=16, at=at):
                target = weights[layer].at[at, low:high, :, first:last]
                pltpu.make_async_copy(source, target, sems.at[layer, at]).start()

            if distance == 0:
                start(whole.at[:, c, other], 0, COLS)
                continue
            begin = REST_AT[distance]
            first = 0 if distance == 2 else ALONG_X
            start(rest.at[:, c, other, :, begin : begin + COLS - first], first, COLS)
            if distance == 2:
                continue
            for own in range(2):

                @pl.when((core == c) == (own == 0))
                def _(own=own, other=other, start=start):
                    early, late = moved[(distance // 2) * 4 + own], moved[(distance // 2) * 4 + 2 + own]
                    start(early.at[:, other], 0, ALONG_X, 0, EARLY)
                    start(late.at[:, other], 0, ALONG_X, EARLY, 16)


def start_layers(order, place, sources, weights, sems):
    x = place[0]
    for layer in order:
        for distance in range(4):

            @pl.when(((x - layer + 4) & 3) == distance)
            def _(layer=layer, distance=distance):
                start_copies(layer, distance, place, sources, weights, sems)


def wait_rows(weights, sems, layer, at):
    block = weights[layer].at[at // CHUNK]
    pltpu.make_async_copy(block, block, sems.at[layer, at // CHUNK]).wait()


def stack_heads(rows):
    return jnp.concatenate([rows[:, h * HEAD : (h + 1) * HEAD] for h in range(HEADS)], axis=0)


def unstack_heads(rows):
    return jnp.concatenate([rows[h * LENGTH : (h + 1) * LENGTH] for h in range(HEADS)], axis=1)


def weight_rows(weights, layer, at, first, last):
    block = weights[layer][at // CHUNK, :, :, first:last]
    return block.reshape(CHUNK, last - first)


def attention_mask(seg_col, seg_row):
    row_ids = lax.broadcasted_iota(jnp.int32, (LENGTH, LENGTH), 0)
    col_ids = lax.broadcasted_iota(jnp.int32, (LENGTH, LENGTH), 1)
    allowed = ((seg_col[...] == seg_row[...]) & (col_ids <= row_ids)).astype(F32)
    return jnp.concatenate([allowed] * HEADS, axis=0) > 0.0


def forward_layers(mask, h_all, kept, out_ref, weights, sems):
    def project(layer, at, rows, acc, squares):
        if sems is not None:
            wait_rows(weights, sems, layer, at)
        wide = rows.astype(F32)
        acc = acc + dot_nn(rows, weight_rows(weights, layer, at, 0, KVW))
        return acc, squares + jnp.sum(wide * wide, axis=-1, keepdims=True)

    start = (jnp.zeros((LENGTH, KVW), F32), jnp.zeros((LENGTH, 1), F32))
    acc, squares = start
    for at in range(0, WIDTH, CHUNK):
        acc, squares = project(0, at, h_all[0, :, at : at + CHUNK], acc, squares)
    for layer in range(LAYERS):
        inverse = lax.rsqrt(squares * (1.0 / WIDTH) + NORM_EPS)
        rows = (acc * inverse).astype(BF16)
        query = stack_heads(rows[:, :QW])
        keys = rows[:, QW : QW + HEAD]
        values = rows[:, QW + HEAD :]
        scores = dot_nt(query, keys) * SCALE
        exp_scores = jnp.where(mask, jnp.exp(scores), 0.0)
        probs = exp_scores / jnp.sum(exp_scores, axis=-1, keepdims=True)
        if kept is not None:
            n_all, i_all, q_all, k_all, v_all, p_all = kept
            for ref, value in zip(kept[2:], (query, keys, values, probs)):
                ref[layer] = value
            i_all[layer] = jnp.broadcast_to(inverse, (LENGTH, HEAD))
            for at in range(0, WIDTH, CHUNK):
                signal = h_all[layer, :, at : at + CHUNK].astype(F32)
                core, side = divmod(at // CHUNK, 2)
                n_all[layer * 4 + side * 2 + core] = (signal * inverse).astype(BF16)
        if out_ref is None and layer + 1 == LAYERS:
            return
        context = unstack_heads(dot_nn(probs.astype(BF16), values).astype(BF16))
        acc, squares = start
        for at in range(0, WIDTH, CHUNK):
            signal = h_all[layer, :, at : at + CHUNK].astype(F32)
            branch = dot_nt(context, weight_rows(weights, layer, at, KVW, COLS))
            result = (signal + branch).astype(BF16)
            if layer + 1 < LAYERS:
                h_all[layer + 1, :, at : at + CHUNK] = result
                acc, squares = project(layer + 1, at, result, acc, squares)
            else:
                out_ref[:, at : at + CHUNK] = result


def backward_layers(need_up, h_all, kept, up, g_all, weights, sems):
    i_all, q_all, k_all, v_all, p_all = kept

    def project(layer, at, rows, acc):
        if sems is not None and layer < LAYERS - LOADED:
            wait_rows(weights, sems, layer, at)
        return acc + dot_nn(rows, weight_rows(weights, layer, at, KVW, COLS))

    acc = jnp.zeros((LENGTH, QW), F32)
    for at in range(0, WIDTH, CHUNK):
        acc = project(LAYERS - 1, at, up[:, at : at + CHUNK], acc)
    for layer in reversed(range(LAYERS)):
        grad_context = stack_heads(acc.astype(BF16))
        query, keys, values, probs = q_all[layer], k_all[layer], v_all[layer], p_all[layer]
        grad_probs = dot_nt(grad_context, values)
        centred = grad_probs - jnp.sum(probs * grad_probs, axis=-1, keepdims=True)
        grad_scores = (probs * centred * SCALE).astype(BF16)
        grad_keys = dot_tn(grad_scores, query).astype(BF16)
        grad_values = dot_tn(probs.astype(BF16), grad_context).astype(BF16)
        if g_all is not None:
            for copy in range(4):
                g_all[layer * 4 + copy, :, :HEAD] = grad_keys
                g_all[layer * 4 + copy, :, HEAD:] = grad_values
        if layer == 0 and not need_up:
            return
        grad_query = dot_nn(grad_scores, keys).astype(BF16)
        grads = jnp.concatenate([unstack_heads(grad_query), grad_keys, grad_values], axis=1)
        by_head = jnp.sum(grad_query.astype(F32) * query.astype(F32), axis=-1, keepdims=True)
        total = sum(by_head[h * LENGTH : (h + 1) * LENGTH] for h in range(HEADS))
        for grad, value in ((grad_keys, keys), (grad_values, values)):
            product = grad.astype(F32) * value.astype(F32)
            total = total + jnp.sum(product, axis=-1, keepdims=True)
        inverse = i_all[layer][:, :1]
        pull = inverse * inverse * (total * (1.0 / WIDTH))
        acc = jnp.zeros((LENGTH, QW), F32)
        for at in range(0, WIDTH, CHUNK):
            part = dot_nt(grads, weight_rows(weights, layer, at, 0, KVW))
            signal = h_all[layer, :, at : at + CHUNK].astype(F32)
            upstream = up[:, at : at + CHUNK].astype(F32)
            result = (upstream + inverse * part - signal * pull).astype(BF16)
            up[:, at : at + CHUNK] = result
            if layer > 0:
                acc = project(layer - 1, at, result, acc)


def first_kernel(place, h_ref, seg_col, seg_row, *refs):
    sources, refs = refs[:SOURCES], refs[SOURCES:]
    out_ref, *weights = refs[: LAYERS + 1]
    h_all, sems = refs[LAYERS + 1 :]
    start_layers(range(LAYERS), place, sources, weights, sems)
    h_all[0] = h_ref[...]
    mask = attention_mask(seg_col, seg_row)
    forward_layers(mask, h_all, None, out_ref, weights, sems)


def middle_kernel(place, h_ref, arrived, up_ref, seg_col, seg_row, *refs):
    weights, refs = refs[:LAYERS], refs[LAYERS:]
    out_ref, h_all, *kept = refs

    @pl.when(place[2] == 1)
    def _():
        h_all[0] = arrived[...]

    @pl.when(place[2] == 0)
    def _():
        h_all[0] = h_ref[...]

    out_ref[...] = up_ref[...]
    mask = attention_mask(seg_col, seg_row)
    forward_layers(mask, h_all, kept, None, weights, None)
    backward_layers(True, h_all, kept[1:], out_ref, None, weights, None)


def load_kernel(place, *refs):
    sources, refs = refs[:SOURCES], refs[SOURCES:]
    *late, sems = refs
    weights = [None] * (LAYERS - LOADED) + late
    layers = range(LAYERS - 1, LAYERS - 1 - LOADED, -1)
    start_layers(layers, place, sources, weights, sems)
    for layer in layers:
        for at in range(0, WIDTH, CHUNK):
            wait_rows(weights, sems, layer, at)


def last_kernel(place, up_ref, arrived, h_all, i_all, q_all, k_all, v_all, p_all, *refs):
    late, refs = refs[:LOADED], refs[LOADED:]
    sources, refs = refs[:SOURCES], refs[SOURCES:]
    g_all, up, sems, *weights = refs
    weights += late
    start_layers(reversed(range(LAYERS - LOADED)), place, sources, weights, sems)

    @pl.when(place[2] == 0)
    def _():
        up[...] = arrived[...]

    @pl.when(place[2] == 1)
    def _():
        up[...] = up_ref[...]

    kept = (i_all, q_all, k_all, v_all, p_all)
    backward_layers(False, h_all, kept, up, g_all, weights, sems)


VM = pl.BlockSpec(memory_space=pltpu.VMEM)
SM = pl.BlockSpec(memory_space=pltpu.SMEM)
ANY = pl.BlockSpec(memory_space=pl.ANY)
WEIGHTS = (pltpu.VMEM((WIDTH // CHUNK, 16, 64, COLS), BF16),) * LAYERS
WEIGHT_SEMS = pltpu.SemaphoreType.DMA((LAYERS, WIDTH // CHUNK))
ROWS = jax.ShapeDtypeStruct((LENGTH, WIDTH), BF16)
ROWS_ALL = pltpu.VMEM((LAYERS, LENGTH, WIDTH), BF16)
STATE_SHAPES = (
    pltpu.HBM((LAYERS, LENGTH, WIDTH), BF16),
    pltpu.HBM((LAYERS * 4, LENGTH, CHUNK), BF16),
    pltpu.HBM((LAYERS, LENGTH, HEAD), F32),
    pltpu.HBM((LAYERS, LENGTH * HEADS, HEAD), BF16),
    pltpu.HBM((LAYERS, LENGTH, HEAD), BF16),
    pltpu.HBM((LAYERS, LENGTH, HEAD), BF16),
    pltpu.HBM((LAYERS, LENGTH * HEADS, LENGTH), F32),
)


def cost(products):
    return pl.CostEstimate(
        flops=products * 2 * LENGTH * WIDTH * COLS,
        bytes_accessed=LAYERS * WIDTH * COLS * 2,
        transcendentals=0,
    )


def call(
    kernel, name, products, out_shape, inputs, sources, scratch, limit=VMEM_LIMIT
):
    return pl.pallas_call(
        kernel,
        out_shape=out_shape,
        in_specs=[SM] + [VM] * (len(inputs) - 1) + [ANY] * len(sources),
        out_specs=(VM,) * len(out_shape),
        scratch_shapes=scratch,
        compiler_params=pltpu.CompilerParams(vmem_limit_bytes=limit),
        cost_estimate=cost(products),
        name=name,
    )(*inputs, *sources)


def reorder(rows):
    split = rows.reshape(LENGTH, 16, 2, 2, 64)
    return split.transpose(0, 3, 2, 1, 4).reshape(LENGTH, WIDTH)


def swap(block, axis):
    return lax.ppermute(block, axis, [(0, 1), (1, 0)])


def turned(block, distance):
    return lax.ppermute(block, "x", [(i, (i + distance) % 4) for i in range(4)])


def across(block):
    return lax.ppermute(block, ("yh", "yl"), [(i, 3 - i) for i in range(4)])


def gather_layers(pair, rest, c):
    whole = lax.all_gather(pair, ("z", "c"), axis=0).reshape(16, 2, 2, 64, COLS)
    edge = rest[:, :, ALONG_X:]
    rest = jnp.concatenate([turned(edge, 1), turned(edge, 3), turned(rest, 2)], axis=2)
    rest = lax.all_gather(rest, ("z", "c"), axis=0).reshape(16, 2, 2, 64, -1)
    share = lax.dynamic_slice(whole, (0, c, 0, 0, 0), (16, 1, 2, 64, ALONG_X))[:, 0]
    early, late = share[:EARLY], share[EARLY:]
    near, far = turned(early, 1), turned(early, 3)
    near, late_near = lax.optimization_barrier((near, late))
    far, late_far = lax.optimization_barrier((far, late))
    near_late, far_late = turned(late_near, 1), turned(late_far, 3)
    moved = []
    for block in (near, near_late, far, far_late):
        moved += [block, swap(block, "c")]
    return [whole, rest] + moved


def sum_over(value, axes, count):
    spread = jnp.broadcast_to(value, (count, 8, 128))
    return jnp.sum(lax.all_to_all(spread, axes, 0, 0, tiled=True), axis=0)


def shards(
    inputs, out_grad, doc_ids, query_weight, out_weight, master, first_moment, second_moment
):
    yh, x, yl, c = (lax.axis_index(name) for name in ("yh", "x", "yl", "c"))
    own = jnp.concatenate(
        [
            query_weight[0],
            master[0, 0].astype(BF16),
            master[0, 1].astype(BF16),
            out_weight[0],
        ],
        axis=1,
    )
    segment = lax.dynamic_index_in_dim(doc_ids, x, 0, keepdims=False)
    rows_in = reorder(lax.dynamic_index_in_dim(inputs, x, 0, keepdims=False))
    up_in = reorder(lax.dynamic_index_in_dim(out_grad, x, 0, keepdims=False))
    up_in = swap(up_in, "yl")
    segment = jnp.where(yh == 1, swap(segment, "yl"), segment)
    seg_col, seg_row = segment[:, None], segment[None, :]
    place = jnp.stack([x, c, yh, yl]).astype(jnp.int32)
    with jax.named_scope("gather_weights"):
        pair = jnp.stack([own, swap(own, "yl")])
        tied = lax.optimization_barrier((pair, place, rows_in, up_in, seg_col, seg_row))
        rest, place, rows_in, up_in, seg_col, seg_row = tied
        sources = gather_layers(pair, rest, c)

    arrived, *weights = call(
        first_kernel,
        "first_forward",
        LAYERS,
        (ROWS,) + WEIGHTS,
        (place, rows_in, seg_col, seg_row),
        sources,
        [ROWS_ALL, WEIGHT_SEMS],
    )
    weights = [pltpu.with_memory_space_constraint(block, pltpu.VMEM) for block in weights]
    arrived = across(arrived)
    half_up, h_all, n_all, *kept = call(
        middle_kernel,
        "second_forward_backward",
        2 * LAYERS,
        (ROWS,) + STATE_SHAPES,
        (place, rows_in, arrived, up_in, seg_col, seg_row, *weights),
        (),
        [],
    )
    with jax.named_scope("normed_slices"):
        rows = lax.all_to_all(n_all, PLANE, 0, 0, tiled=True).reshape(-1, CHUNK)
    arrived = across(half_up)
    place, _ = lax.optimization_barrier((place, half_up))
    late = call(
        load_kernel,
        "load_weights",
        LOADED,
        WEIGHTS[:LOADED],
        (place,),
        sources,
        [WEIGHT_SEMS],
    )
    late = [pltpu.with_memory_space_constraint(block, pltpu.VMEM) for block in late]
    (grads,) = call(
        last_kernel,
        "first_backward",
        LAYERS,
        (jax.ShapeDtypeStruct((LAYERS * 4, LENGTH, 2 * HEAD), BF16),),
        (place, up_in, arrived, h_all, *kept, *late),
        sources,
        [pltpu.VMEM((LENGTH, WIDTH), BF16), WEIGHT_SEMS, *WEIGHTS[LOADED:]],
        VMEM_LAST,
    )

    with jax.named_scope("gather_grads"):
        grads, rows = lax.optimization_barrier((grads, rows))
        cols = lax.all_to_all(grads, PLANE, 0, 0, tiled=True).reshape(-1, 2 * HEAD)

    with jax.named_scope("sum_grads"):
        partial = dot_tn(rows, cols).astype(BF16).reshape(16, 64, 2 * HEAD)
        parts = lax.all_to_all(partial, "z", 0, 0, tiled=True)
        grad = jnp.sum(parts.astype(F32), axis=0)
        grad = jnp.stack([grad[:, :HEAD], grad[:, HEAD:]])

    with jax.named_scope("clip"):
        total_sq = sum_over(jnp.sum(grad * grad), "z", 16)
        total_sq = sum_over(total_sq, ("yh",) + PLANE, 32)
        factor = jnp.minimum(1.0, CLIP_NORM / jnp.sqrt(total_sq[0, 0]))
    clipped = grad * factor
    first_new = BETA_FIRST * first_moment[0] + (1.0 - BETA_FIRST) * clipped
    second_new = BETA_SECOND * second_moment[0] + (1.0 - BETA_SECOND) * clipped * clipped
    adam_step = first_new / (jnp.sqrt(second_new) + ADAM_EPSILON)
    fresh_shard = (master[0] - LEARN_RATE * adam_step).astype(BF16)
    return (adam_step[None], fresh_shard[None])


def solution(mesh):
    fine = Mesh(mesh.devices.reshape(tuple(FINE.values())), tuple(FINE))
    section = ("yh", "x")
    placed = (
        P(None, DP, None),
        P(None, DP, None),
        P(None, DP),
        P(section, DP, None),
        P(section, DP, None),
        P(section, None, DP, None),
        P(section, None, DP, None),
        P(section, None, DP, None),
    )
    return jax.shard_map(
        shards,
        mesh=fine,
        in_specs=placed,
        out_specs=(P(section, None, DP, None), P(section, None, DP, None)),
        check_vma=False,
    )
```

```python
import functools
import math

import jax
import jax.numpy as jnp
from jax import lax
from jax.experimental import pallas as pl
from jax.experimental.pallas import tpu as pltpu
from jax.sharding import Mesh, PartitionSpec as P

NORM_EPS = 1e-05
BETA_FIRST = 0.9
BETA_SECOND = 0.95
ADAM_EPSILON = 1e-08
LEARN_RATE = 0.001
CLIP_NORM = 1.0

FINE = {"yh": 2, "x": 4, "zh": 8, "zl": 2, "yl": 2, "c": 2}
Z = ("zh", "zl")
DP = Z + ("yl", "c")
NEAR = ("x", "zl", "yl", "c")
LAYERS = 4
LENGTH = 32
WIDTH = 4096
HEAD = 128
HEADS = 4
QW = HEAD * HEADS
KVW = QW + 2 * HEAD
COLS = KVW + QW
CHUNK = 1024
LOADED = 1
ALONG_X = 896
EARLY = 10
REST_AT = {1: 0, 3: COLS - ALONG_X, 2: 2 * (COLS - ALONG_X)}
SOURCES = 10
SCALE = 1.0 / math.sqrt(HEAD)
VMEM_LIMIT = 7 * 1024 * 1024
VMEM_LAST = 37 * 1024 * 1024
F32 = jnp.float32
BF16 = jnp.bfloat16


def dot_nn(a, b):
    return lax.dot_general(a, b, (((1,), (0,)), ((), ())), preferred_element_type=F32)


def dot_nt(a, b):
    return lax.dot_general(a, b, (((1,), (1,)), ((), ())), preferred_element_type=F32)


def dot_tn(a, b):
    return lax.dot_general(a, b, (((0,), (0,)), ((), ())), preferred_element_type=F32)


def start_copies(layer, distance, place, sources, weights, sems):
    whole, rest, *moved = sources
    core, side = place[1], place[3]
    for c in range(2):
        for other in range(2):
            at = c * 2 + (side if other == 0 else 1 - side)

            def start(source, first, last, low=0, high=16, at=at):
                target = weights[layer].at[at, low:high, :, first:last]
                pltpu.make_async_copy(source, target, sems.at[layer, at]).start()

            if distance == 0:
                start(whole.at[:, c, other], 0, COLS)
                continue
            begin = REST_AT[distance]
            first = 0 if distance == 2 else ALONG_X
            start(rest.at[:, c, other, :, begin : begin + COLS - first], first, COLS)
            if distance == 2:
                continue
            for own in range(2):

                @pl.when((core == c) == (own == 0))
                def _(own=own, other=other, start=start):
                    early, late = moved[(distance // 2) * 4 + own], moved[(distance // 2) * 4 + 2 + own]
                    start(early.at[:, other], 0, ALONG_X, 0, EARLY)
                    start(late.at[:, other], 0, ALONG_X, EARLY, 16)


def start_layers(order, place, sources, weights, sems):
    x = place[0]
    for layer in order:
        for distance in range(4):

            @pl.when(((x - layer + 4) & 3) == distance)
            def _(layer=layer, distance=distance):
                start_copies(layer, distance, place, sources, weights, sems)


def wait_rows(weights, sems, layer, at):
    block = weights[layer].at[at // CHUNK]
    pltpu.make_async_copy(block, block, sems.at[layer, at // CHUNK]).wait()


def stack_heads(rows):
    return jnp.concatenate([rows[:, h * HEAD : (h + 1) * HEAD] for h in range(HEADS)], axis=0)


def unstack_heads(rows):
    return jnp.concatenate([rows[h * LENGTH : (h + 1) * LENGTH] for h in range(HEADS)], axis=1)


def weight_rows(weights, layer, at, first, last):
    block = weights[layer][at // CHUNK, :, :, first:last]
    return block.reshape(CHUNK, last - first)


def attention_mask(seg_col, seg_row):
    row_ids = lax.broadcasted_iota(jnp.int32, (LENGTH, LENGTH), 0)
    col_ids = lax.broadcasted_iota(jnp.int32, (LENGTH, LENGTH), 1)
    allowed = ((seg_col[...] == seg_row[...]) & (col_ids <= row_ids)).astype(F32)
    return jnp.concatenate([allowed] * HEADS, axis=0) > 0.0


def forward_layers(mask, h_all, kept, out_ref, weights, sems):
    def project(layer, at, rows, acc, squares):
        if sems is not None:
            wait_rows(weights, sems, layer, at)
        wide = rows.astype(F32)
        acc = acc + dot_nn(rows, weight_rows(weights, layer, at, 0, KVW))
        return acc, squares + jnp.sum(wide * wide, axis=-1, keepdims=True)

    start = (jnp.zeros((LENGTH, KVW), F32), jnp.zeros((LENGTH, 1), F32))
    acc, squares = start
    for at in range(0, WIDTH, CHUNK):
        acc, squares = project(0, at, h_all[0, :, at : at + CHUNK], acc, squares)
    for layer in range(LAYERS):
        inverse = lax.rsqrt(squares * (1.0 / WIDTH) + NORM_EPS)
        rows = (acc * inverse).astype(BF16)
        query = stack_heads(rows[:, :QW])
        keys = rows[:, QW : QW + HEAD]
        values = rows[:, QW + HEAD :]
        scores = dot_nt(query, keys) * SCALE
        exp_scores = jnp.where(mask, jnp.exp(scores), 0.0)
        probs = exp_scores / jnp.sum(exp_scores, axis=-1, keepdims=True)
        if kept is not None:
            n_all, i_all, q_all, k_all, v_all, p_all = kept
            for ref, value in zip(kept[2:], (query, keys, values, probs)):
                ref[layer] = value
            i_all[layer] = jnp.broadcast_to(inverse, (LENGTH, HEAD))
            for at in range(0, WIDTH, CHUNK):
                signal = h_all[layer, :, at : at + CHUNK].astype(F32)
                core, side = divmod(at // CHUNK, 2)
                normed = (signal * inverse).astype(BF16)
                for pair in range(2):
                    n_all[layer * 8 + pair * 4 + side * 2 + core] = normed
        if out_ref is None and layer + 1 == LAYERS:
            return
        context = unstack_heads(dot_nn(probs.astype(BF16), values).astype(BF16))
        acc, squares = start
        for at in range(0, WIDTH, CHUNK):
            signal = h_all[layer, :, at : at + CHUNK].astype(F32)
            branch = dot_nt(context, weight_rows(weights, layer, at, KVW, COLS))
            result = (signal + branch).astype(BF16)
            if layer + 1 < LAYERS:
                h_all[layer + 1, :, at : at + CHUNK] = result
                acc, squares = project(layer + 1, at, result, acc, squares)
            else:
                out_ref[:, at : at + CHUNK] = result


def backward_layers(need_up, h_all, kept, up, g_all, weights, sems):
    i_all, q_all, k_all, v_all, p_all = kept

    def project(layer, at, rows, acc):
        if sems is not None and layer < LAYERS - LOADED:
            wait_rows(weights, sems, layer, at)
        return acc + dot_nn(rows, weight_rows(weights, layer, at, KVW, COLS))

    acc = jnp.zeros((LENGTH, QW), F32)
    for at in range(0, WIDTH, CHUNK):
        acc = project(LAYERS - 1, at, up[:, at : at + CHUNK], acc)
    for layer in reversed(range(LAYERS)):
        grad_context = stack_heads(acc.astype(BF16))
        query, keys, values, probs = q_all[layer], k_all[layer], v_all[layer], p_all[layer]
        grad_probs = dot_nt(grad_context, values)
        centred = grad_probs - jnp.sum(probs * grad_probs, axis=-1, keepdims=True)
        grad_scores = (probs * centred * SCALE).astype(BF16)
        grad_keys = dot_tn(grad_scores, query).astype(BF16)
        grad_values = dot_tn(probs.astype(BF16), grad_context).astype(BF16)
        if g_all is not None:
            for copy in range(4):
                g_all[layer * 8 + copy] = grad_keys
                g_all[layer * 8 + 4 + copy] = grad_values
        if layer == 0 and not need_up:
            return
        grad_query = dot_nn(grad_scores, keys).astype(BF16)
        grads = jnp.concatenate([unstack_heads(grad_query), grad_keys, grad_values], axis=1)
        by_head = jnp.sum(grad_query.astype(F32) * query.astype(F32), axis=-1, keepdims=True)
        total = sum(by_head[h * LENGTH : (h + 1) * LENGTH] for h in range(HEADS))
        for grad, value in ((grad_keys, keys), (grad_values, values)):
            product = grad.astype(F32) * value.astype(F32)
            total = total + jnp.sum(product, axis=-1, keepdims=True)
        inverse = i_all[layer][:, :1]
        pull = inverse * inverse * (total * (1.0 / WIDTH))
        acc = jnp.zeros((LENGTH, QW), F32)
        for at in range(0, WIDTH, CHUNK):
            part = dot_nt(grads, weight_rows(weights, layer, at, 0, KVW))
            signal = h_all[layer, :, at : at + CHUNK].astype(F32)
            upstream = up[:, at : at + CHUNK].astype(F32)
            result = (upstream + inverse * part - signal * pull).astype(BF16)
            up[:, at : at + CHUNK] = result
            if layer > 0:
                acc = project(layer - 1, at, result, acc)


def first_kernel(place, h_ref, seg_col, seg_row, *refs):
    sources, refs = refs[:SOURCES], refs[SOURCES:]
    out_ref, *weights = refs[: LAYERS + 1]
    h_all, sems = refs[LAYERS + 1 :]
    start_layers(range(LAYERS), place, sources, weights, sems)
    h_all[0] = h_ref[...]
    mask = attention_mask(seg_col, seg_row)
    forward_layers(mask, h_all, None, out_ref, weights, sems)


def middle_kernel(place, h_ref, arrived, up_ref, seg_col, seg_row, *refs):
    weights, refs = refs[:LAYERS], refs[LAYERS:]
    out_ref, h_all, *kept = refs

    @pl.when(place[2] == 1)
    def _():
        h_all[0] = arrived[...]

    @pl.when(place[2] == 0)
    def _():
        h_all[0] = h_ref[...]

    out_ref[...] = up_ref[...]
    mask = attention_mask(seg_col, seg_row)
    forward_layers(mask, h_all, kept, None, weights, None)
    backward_layers(True, h_all, kept[1:], out_ref, None, weights, None)


def load_kernel(place, *refs):
    sources, refs = refs[:SOURCES], refs[SOURCES:]
    *late, sems = refs
    weights = [None] * (LAYERS - LOADED) + late
    layers = range(LAYERS - 1, LAYERS - 1 - LOADED, -1)
    start_layers(layers, place, sources, weights, sems)
    for layer in layers:
        for at in range(0, WIDTH, CHUNK):
            wait_rows(weights, sems, layer, at)


def last_kernel(place, up_ref, arrived, h_all, i_all, q_all, k_all, v_all, p_all, *refs):
    late, refs = refs[:LOADED], refs[LOADED:]
    sources, refs = refs[:SOURCES], refs[SOURCES:]
    g_all, up, sems, *weights = refs
    weights += late
    start_layers(reversed(range(LAYERS - LOADED)), place, sources, weights, sems)

    @pl.when(place[2] == 0)
    def _():
        up[...] = arrived[...]

    @pl.when(place[2] == 1)
    def _():
        up[...] = up_ref[...]

    kept = (i_all, q_all, k_all, v_all, p_all)
    backward_layers(False, h_all, kept, up, g_all, weights, sems)


VM = pl.BlockSpec(memory_space=pltpu.VMEM)
SM = pl.BlockSpec(memory_space=pltpu.SMEM)
ANY = pl.BlockSpec(memory_space=pl.ANY)
WEIGHTS = (pltpu.VMEM((WIDTH // CHUNK, 16, 64, COLS), BF16),) * LAYERS
WEIGHT_SEMS = pltpu.SemaphoreType.DMA((LAYERS, WIDTH // CHUNK))
ROWS = jax.ShapeDtypeStruct((LENGTH, WIDTH), BF16)
ROWS_ALL = pltpu.VMEM((LAYERS, LENGTH, WIDTH), BF16)
STATE_SHAPES = (
    pltpu.HBM((LAYERS, LENGTH, WIDTH), BF16),
    pltpu.HBM((LAYERS * 8, LENGTH, CHUNK), BF16),
    pltpu.HBM((LAYERS, LENGTH, HEAD), F32),
    pltpu.HBM((LAYERS, LENGTH * HEADS, HEAD), BF16),
    pltpu.HBM((LAYERS, LENGTH, HEAD), BF16),
    pltpu.HBM((LAYERS, LENGTH, HEAD), BF16),
    pltpu.HBM((LAYERS, LENGTH * HEADS, LENGTH), F32),
)


def cost(products):
    return pl.CostEstimate(
        flops=products * 2 * LENGTH * WIDTH * COLS,
        bytes_accessed=LAYERS * WIDTH * COLS * 2,
        transcendentals=0,
    )


def call(
    kernel, name, products, out_shape, inputs, sources, scratch, limit=VMEM_LIMIT
):
    return pl.pallas_call(
        kernel,
        out_shape=out_shape,
        in_specs=[SM] + [VM] * (len(inputs) - 1) + [ANY] * len(sources),
        out_specs=(VM,) * len(out_shape),
        scratch_shapes=scratch,
        compiler_params=pltpu.CompilerParams(vmem_limit_bytes=limit),
        cost_estimate=cost(products),
        name=name,
    )(*inputs, *sources)


def reorder(rows):
    split = rows.reshape(LENGTH, 16, 2, 2, 64)
    return split.transpose(0, 3, 2, 1, 4).reshape(LENGTH, WIDTH)


def swap(block, axis):
    return lax.ppermute(block, axis, [(0, 1), (1, 0)])


def turned(block, distance):
    return lax.ppermute(block, "x", [(i, (i + distance) % 4) for i in range(4)])


def across(block):
    return lax.ppermute(block, ("yh", "yl"), [(i, 3 - i) for i in range(4)])


def gather_layers(pair, rest, c):
    whole = lax.all_gather(pair, Z + ("c",), axis=0).reshape(16, 2, 2, 64, COLS)
    edge = rest[:, :, ALONG_X:]
    rest = jnp.concatenate([turned(edge, 1), turned(edge, 3), turned(rest, 2)], axis=2)
    rest = lax.all_gather(rest, Z + ("c",), axis=0).reshape(16, 2, 2, 64, -1)
    share = lax.dynamic_slice(whole, (0, c, 0, 0, 0), (16, 1, 2, 64, ALONG_X))[:, 0]
    early, late = share[:EARLY], share[EARLY:]
    near, far = turned(early, 1), turned(early, 3)
    near, late_near = lax.optimization_barrier((near, late))
    far, late_far = lax.optimization_barrier((far, late))
    near_late, far_late = turned(late_near, 1), turned(late_far, 3)
    moved = []
    for block in (near, near_late, far, far_late):
        moved += [block, swap(block, "c")]
    return [whole, rest] + moved


def sum_over(value, axes, count):
    spread = jnp.broadcast_to(value, (count, 8, 128))
    return jnp.sum(lax.all_to_all(spread, axes, 0, 0, tiled=True), axis=0)


def shards(
    inputs, out_grad, doc_ids, query_weight, out_weight, master, first_moment, second_moment
):
    yh, x, zl, yl, c = (lax.axis_index(name) for name in ("yh", "x", "zl", "yl", "c"))
    own = jnp.concatenate(
        [
            query_weight[0],
            master[0, 0].astype(BF16),
            master[0, 1].astype(BF16),
            out_weight[0],
        ],
        axis=1,
    )
    segment = lax.dynamic_index_in_dim(doc_ids, x, 0, keepdims=False)
    rows_in = reorder(lax.dynamic_index_in_dim(inputs, x, 0, keepdims=False))
    up_in = reorder(lax.dynamic_index_in_dim(out_grad, x, 0, keepdims=False))
    up_in = swap(up_in, "yl")
    segment = jnp.where(yh == 1, swap(segment, "yl"), segment)
    seg_col, seg_row = segment[:, None], segment[None, :]
    place = jnp.stack([x, c, yh, yl]).astype(jnp.int32)
    with jax.named_scope("gather_weights"):
        pair = jnp.stack([own, swap(own, "yl")])
        tied = lax.optimization_barrier((pair, place, rows_in, up_in, seg_col, seg_row))
        rest, place, rows_in, up_in, seg_col, seg_row = tied
        sources = gather_layers(pair, rest, c)

    arrived, *weights = call(
        first_kernel,
        "first_forward",
        LAYERS,
        (ROWS,) + WEIGHTS,
        (place, rows_in, seg_col, seg_row),
        sources,
        [ROWS_ALL, WEIGHT_SEMS],
    )
    weights = [pltpu.with_memory_space_constraint(block, pltpu.VMEM) for block in weights]
    arrived = across(arrived)
    half_up, h_all, n_all, *kept = call(
        middle_kernel,
        "second_forward_backward",
        2 * LAYERS,
        (ROWS,) + STATE_SHAPES,
        (place, rows_in, arrived, up_in, seg_col, seg_row, *weights),
        (),
        [],
    )
    with jax.named_scope("normed_slices"):
        rows = lax.all_to_all(n_all, NEAR, 0, 0, tiled=True).reshape(-1, CHUNK)
    arrived = across(half_up)
    place, _ = lax.optimization_barrier((place, half_up))
    late = call(
        load_kernel,
        "load_weights",
        LOADED,
        WEIGHTS[:LOADED],
        (place,),
        sources,
        [WEIGHT_SEMS],
    )
    late = [pltpu.with_memory_space_constraint(block, pltpu.VMEM) for block in late]
    (grads,) = call(
        last_kernel,
        "first_backward",
        LAYERS,
        (jax.ShapeDtypeStruct((LAYERS * 8, LENGTH, HEAD), BF16),),
        (place, up_in, arrived, h_all, *kept, *late),
        sources,
        [pltpu.VMEM((LENGTH, WIDTH), BF16), WEIGHT_SEMS, *WEIGHTS[LOADED:]],
        VMEM_LAST,
    )

    with jax.named_scope("gather_grads"):
        grads, rows = lax.optimization_barrier((grads, rows))
        cols = lax.all_to_all(grads, NEAR, 0, 0, tiled=True).reshape(-1, HEAD)

    with jax.named_scope("sum_grads"):
        partial = dot_tn(rows, cols).astype(BF16).reshape(8, 128, HEAD)
        parts = lax.all_to_all(partial, "zh", 0, 0, tiled=True)
        both = jnp.sum(parts.astype(F32), axis=0)
        mine = lax.dynamic_slice_in_dim(both, zl * 64, 64, 0)
        other = swap(lax.dynamic_slice_in_dim(both, (1 - zl) * 64, 64, 0), "zl")
        grad = jnp.stack([jnp.where(zl == 0, mine, other), jnp.where(zl == 0, other, mine)])

    with jax.named_scope("clip"):
        total_sq = sum_over(jnp.sum(both * both), Z, 16)
        total_sq = sum_over(total_sq, ("yh", "x", "yl", "c"), 32)
        factor = jnp.minimum(1.0, CLIP_NORM / jnp.sqrt(total_sq[0, 0]))
    clipped = grad * factor
    first_new = BETA_FIRST * first_moment[0] + (1.0 - BETA_FIRST) * clipped
    second_new = BETA_SECOND * second_moment[0] + (1.0 - BETA_SECOND) * clipped * clipped
    adam_step = first_new / (jnp.sqrt(second_new) + ADAM_EPSILON)
    fresh_shard = (master[0] - LEARN_RATE * adam_step).astype(BF16)
    return (adam_step[None], fresh_shard[None])


def solution(mesh):
    fine = Mesh(mesh.devices.reshape(tuple(FINE.values())), tuple(FINE))
    section = ("yh", "x")
    placed = (
        P(None, DP, None),
        P(None, DP, None),
        P(None, DP),
        P(section, DP, None),
        P(section, DP, None),
        P(section, None, DP, None),
        P(section, None, DP, None),
        P(section, None, DP, None),
    )
    return jax.shard_map(
        shards,
        mesh=fine,
        in_specs=placed,
        out_specs=(P(section, None, DP, None), P(section, None, DP, None)),
        check_vma=False,
    )
```
